32 devices in a mesh: section: 2 (over x), dp: 4 (over z), tensor: 4 (over y, core).
Axes of the slice: x: 2, y: 2, z: 4, core: 2. Of those that a mesh axis runs over, the one named last changes fastest.
Arguments:
- table_input: bfloat16 [8, 1024, 1024], P('dp'), may hold values from -6 to 6
- target_input: bfloat16 [8, 128, 1024], P('dp'), may hold values from -6 to 6
- cotangent: bfloat16 [8, 128, 1024], P('dp'), may hold values from -6 to 6
- table_lengths: int32 [8], P('dp'), may hold values from 51 to 1024, as said below
- target_lengths: int32 [8], P('dp'), may hold values from 16 to 128, as said below
- query_key: bfloat16 [2, 3, 1024, 1024], P('section', None, None, 'tensor'), may hold values from -0.1875 to 0.1875
- value_out: bfloat16 [2, 3, 1024, 1024], P('section', None, None, 'tensor'), may hold values from -0.5 to 0.5
- hidden_in: bfloat16 [2, 1024, 4096], P('section', None, 'tensor'), may hold values from -0.1875 to 0.1875
- hidden_out: bfloat16 [2, 1024, 4096], P('section', None, 'tensor'), may hold values from -0.125 to 0.125
- hidden_bias: float32 [2, 4096], P('section', 'tensor'), may hold values from -3 to 3
- vectors: float32 [2, 11, 1024], P('section'), may hold values from -2 to 2
- cross_bias: float32 [1024], replicated, may hold values from -3 to 3
Outputs:
- decoded: bfloat16 [8, 128, 1024], P('dp', ('section', 'tensor'))
- table_grad: bfloat16 [8, 1024, 1024], P('dp', ('section', 'tensor'))
- target_grad: bfloat16 [8, 128, 1024], P('dp', ('section', 'tensor'))
- query_key_grad: float32 [2, 3, 1024, 1024], P('section', None, None, 'tensor')
- value_out_grad: float32 [2, 3, 1024, 1024], P('section', None, None, 'tensor')
- hidden_in_grad: float32 [2, 1024, 4096], P('section', None, 'tensor')
- hidden_out_grad: float32 [2, 1024, 4096], P('section', None, 'tensor')
- hidden_bias_grad: float32 [2, 4096], P('section', 'tensor')
- vectors_grad: float32 [2, 11, 1024], P('section')
- cross_bias_grad: float32 [1024], replicated
The draws below stay inside these ranges and needn't reach their ends.
Inputs may be any that keep to these rules, and one draw needn't show every extreme that they name: `table_lengths`: each aligned block of 2 tables (the tables of one index of dp) holds a table of exactly 1024 tokens. `target_lengths`: each aligned block of 2 targets (those of one index of dp) holds one of exactly 128 tokens.
All inputs are finite; a program needn't handle non-finite values.
Results may differ from the reference program's by a relative error of at most 0.034.
Values may be sent and summed in bfloat16 or wider, within the bound.
No kernel may reach another device: no remote copies, remote signals or barrier semaphores. Data moves between devices by JAX's collectives and lax.ppermute only.
A program may use at most 192 MiB of HBM per device.

```python
import jax
import jax.numpy as jnp
from jax import lax

D = 1024
HEAD = 64
FF = 4096
L_ENC = 1024
TGT = 128
TB = 1
MB = 2
TABLES = 8


def draw_table_lengths(key, part):
    key = jax.random.fold_in(key, 11)
    base_key, pick_key = jax.random.split(key)
    block = TB * MB
    lengths = jax.random.randint(base_key, (TABLES,), max(L_ENC // 20, 1), L_ENC + 1)
    chosen = jax.random.randint(pick_key, (TABLES // block, 1), 0, block)
    longest = (jnp.arange(block)[None, :] == chosen).reshape(TABLES)
    return jnp.where(longest, L_ENC, lengths).astype(jnp.int32)


def draw_target_lengths(key, part):
    key = jax.random.fold_in(key, 13)
    base_key, pick_key = jax.random.split(key)
    block = TB * MB
    lengths = jax.random.randint(base_key, (TABLES,), max(TGT // 8, 1), TGT + 1)
    chosen = jax.random.randint(pick_key, (TABLES // block, 1), 0, block)
    longest = (jnp.arange(block)[None, :] == chosen).reshape(TABLES)
    return jnp.where(longest, TGT, lengths).astype(jnp.int32)


def draw_vectors(key, part):
    key = jax.random.fold_in(key, 17)
    gain_key, shift_key = jax.random.split(key)
    row_index = jnp.arange(11)[None, :, None]
    is_gain = (row_index == 5) | (row_index == 7) | (row_index == 9)
    gain_draw = jax.random.uniform(gain_key, (2, 11, D), jnp.float32, 0.5, 1.5)
    shifts = jnp.clip(0.5 * jax.random.normal(shift_key, (2, 11, D), jnp.float32), -2.0, 2.0)
    return jnp.where(is_gain, gain_draw, shifts)


def levels(key, extent, cuts, low, top_value):
    factor_of, own = 1.0, jax.random.fold_in(key, 6)
    for axis_at, blocks in cuts:
        steps = jnp.exp(jax.random.uniform(jax.random.fold_in(own, axis_at), (blocks,), jnp.float32, low / len(cuts), top_value / len(cuts)))
        factor_of = factor_of * jnp.repeat(steps, extent[axis_at] // blocks).reshape([-1 if axis == axis_at else 1 for axis in range(len(extent))])
    return factor_of


def scatter_about(rng, extent, deviation, reach, cuts=(), dtype=jnp.bfloat16):
    loudness = levels(rng, extent, cuts, -0.22, 0.18) if cuts else 1.0
    entries = jax.random.normal(rng, extent, jnp.float32) * deviation * loudness
    return jnp.minimum(jnp.maximum(entries, -reach), reach).astype(dtype)


def setup_inputs(seed: int = 0) -> dict:
    streams_of = jax.random.split(jax.random.key(seed), 13)
    table_input = scatter_about(streams_of[0], (TABLES, L_ENC, D), 1.0, 6.0, ((0, 4),))
    target_input = scatter_about(streams_of[1], (TABLES, TGT, D), 1.0, 6.0, ((0, 4),))
    cotangent = scatter_about(streams_of[2], (TABLES, TGT, D), 1.0, 6.0, ((0, 4),))
    table_lengths = draw_table_lengths(jax.random.fold_in(streams_of[12], 71), 0)
    target_lengths = draw_target_lengths(jax.random.fold_in(streams_of[12], 71), 0)
    query_key = scatter_about(streams_of[5], (2, 3, D, D), D ** -0.5, 0.1875, ((0, 2), (3, 4)))
    value_out = scatter_about(streams_of[6], (2, 3, D, D), (D // 8) ** -0.5, 0.5, ((0, 2), (3, 4)))
    hidden_in = scatter_about(streams_of[7], (2, D, FF), D ** -0.5, 0.1875, ((0, 2), (2, 4)))
    hidden_out = scatter_about(streams_of[8], (2, D, FF), (FF // 2) ** -0.5, 0.125, ((0, 2), (2, 4)))
    hidden_bias = scatter_about(streams_of[9], (2, FF), 0.5, 3.0, ((0, 2), (1, 4)), jnp.float32)
    vectors = draw_vectors(jax.random.fold_in(streams_of[12], 71), 0)
    cross_bias = scatter_about(streams_of[11], (D,), 0.5, 3.0, (), jnp.float32)
    return {"table_input": table_input, "target_input": target_input, "cotangent": cotangent, "table_lengths": table_lengths, "target_lengths": target_lengths, "query_key": query_key, "value_out": value_out, "hidden_in": hidden_in, "hidden_out": hidden_out, "hidden_bias": hidden_bias, "vectors": vectors, "cross_bias": cross_bias}


epsilon = 1e-05
highest = lax.Precision.HIGHEST

@jax.custom_vjp
def low(v):
    return lax.optimization_barrier(v.astype(jnp.bfloat16)).astype(jnp.float32)

@jax.custom_vjp
def low_back(v):
    return v

def low_keep(v):
    return (low(v), None)

def low_pass(kept, grad):
    return (grad,)

def back_keep(v):
    return (v, None)

def back_low(kept, grad):
    return (low(grad),)
low.defvjp(low_keep, low_pass)
low_back.defvjp(back_keep, back_low)

def layer_norm(summed, norm_gain, norm_shift):
    centered = summed - lax.optimization_barrier(jnp.mean(summed, axis=-1, keepdims=True))
    spread = lax.optimization_barrier(jnp.mean(centered * centered, axis=-1, keepdims=True))
    return centered * lax.rsqrt(spread + epsilon) * norm_gain + norm_shift

def project(inputs, matrix):
    return jnp.einsum('gld,dk->glk', inputs, matrix, precision=highest)

def project_back(inputs, matrix):
    return jnp.einsum('glk,dk->gld', inputs, matrix, precision=highest)

def attend(queries, key_rows, value_rows, key_valid, causal):
    tables, query_count, features = queries.shape
    head_count = features // HEAD
    block_rows = min(512, query_count)
    scaling = HEAD ** (-0.5)
    query_blocks = jnp.moveaxis(queries.reshape(tables, query_count // block_rows, block_rows, head_count, HEAD), 1, 0)
    key_split = key_rows.reshape(tables, -1, head_count, HEAD)
    value_split = value_rows.reshape(tables, -1, head_count, HEAD)
    starts = jnp.arange(query_count // block_rows) * block_rows

    def one_block(pieces):
        query_part, start_row = pieces
        scores = low_back(jnp.einsum('gqhe,gkhe->ghqk', query_part, key_split, precision=highest) * scaling)
        allowed = key_valid[:, None, None, :]
        if causal:
            query_rows = start_row + jnp.arange(block_rows)[:, None]
            key_index = jnp.arange(key_valid.shape[1])[None, :]
            allowed = allowed & (key_index <= query_rows)[None, None]
        scores = jnp.where(allowed, scores, -1e+30)
        largest = lax.optimization_barrier(jnp.max(scores, axis=-1, keepdims=True))
        exponent = jnp.exp(scores - largest)
        weights = low(exponent / lax.optimization_barrier(jnp.sum(exponent, axis=-1, keepdims=True)))
        return jnp.einsum('ghqk,gkhe->gqhe', weights, value_split, precision=highest)
    outputs = lax.map(jax.checkpoint(one_block), (query_blocks, starts))
    return jnp.moveaxis(outputs, 0, 1).reshape(tables, query_count, features)

def self_block(inputs, query_key, value_out, vector_rows, key_valid, causal):
    queries = low(low_back(project(inputs, query_key[0]) + vector_rows[0]))
    key_rows = low(low_back(project(inputs, query_key[1])))
    value_rows = low(low_back(project(inputs, value_out[0]) + vector_rows[1]))
    outputs = low(low_back(attend(queries, key_rows, value_rows, key_valid, causal)))
    return low_back(project_back(outputs, value_out[1]))

def ffn_block(inputs, hidden_in, hidden_out, hidden_bias):
    before = low_back(project(low(inputs), hidden_in) + hidden_bias)
    hidden = low(jax.nn.gelu(before, approximate=False))
    return low_back(project_back(hidden, hidden_out))

def layers(table_rows, target_rows, table_valid, target_valid, query_key, value_out, hidden_in, hidden_out, hidden_bias, vectors, cross_bias):
    first_vec = vectors[0]
    normed = layer_norm(table_rows, first_vec[9], first_vec[10])
    branch = self_block(low(normed), query_key[0], value_out[0], first_vec, table_valid, False)
    middle = layer_norm(normed + branch + first_vec[3], first_vec[5], first_vec[6])
    memory = layer_norm(middle + ffn_block(middle, hidden_in[0], hidden_out[0], hidden_bias[0]) + first_vec[4], first_vec[7], first_vec[8])
    memory_low = low(memory)
    cross_keys = low(low_back(project(memory_low, query_key[0, 2])))
    cross_values = low(low_back(project(memory_low, value_out[0, 2]) + first_vec[2]))
    second_vec = vectors[1]
    branch = self_block(low(target_rows), query_key[1], value_out[1], second_vec, target_valid, True)
    upper = layer_norm(target_rows + branch + second_vec[3], second_vec[5], second_vec[6])
    cross_queries = low(low_back(project(low(upper), query_key[1, 2]) + second_vec[2]))
    cross_heads = low(low_back(attend(cross_queries, cross_keys, cross_values, table_valid, False)))
    later = layer_norm(upper + low_back(project_back(cross_heads, value_out[1, 2])) + cross_bias, second_vec[9], second_vec[10])
    return layer_norm(later + ffn_block(later, hidden_in[1], hidden_out[1], hidden_bias[1]) + second_vec[4], second_vec[7], second_vec[8])

def reference(table_input, target_input, cotangent, table_lengths, target_lengths, query_key, value_out, hidden_in, hidden_out, hidden_bias, vectors, cross_bias):
    params = (query_key.astype(jnp.float32), value_out.astype(jnp.float32), hidden_in.astype(jnp.float32), hidden_out.astype(jnp.float32), hidden_bias.astype(jnp.float32), vectors.astype(jnp.float32), cross_bias.astype(jnp.float32))
    group_count = TABLES // TB

    def grouped(values_in):
        return values_in.reshape((group_count, TB) + values_in.shape[1:])

    def one_group(totals, pieces):
        table_rows, target_rows, grad_rows, table_count, target_count = pieces
        table_valid = jnp.arange(L_ENC)[None, :] < table_count[:, None]
        target_valid = jnp.arange(TGT)[None, :] < target_count[:, None]

        def forward(table_part, target_part, *weights):
            return layers(table_part, target_part, table_valid, target_valid, *weights)
        decoded, pull_back = jax.vjp(forward, table_rows.astype(jnp.float32), target_rows.astype(jnp.float32), *params)
        grads = pull_back(grad_rows.astype(jnp.float32))
        totals = tuple((running + update for running, update in zip(totals, grads[2:])))
        return (totals, (decoded.astype(jnp.bfloat16), grads[0].astype(jnp.bfloat16), grads[1].astype(jnp.bfloat16)))
    start = tuple((jnp.zeros(param.shape, jnp.float32) for param in params))
    totals, outputs = lax.scan(one_group, start, (grouped(table_input), grouped(target_input), grouped(cotangent), grouped(table_lengths), grouped(target_lengths)))
    decoded, table_grad, target_grad = outputs
    return (decoded.reshape(TABLES, TGT, D), table_grad.reshape(TABLES, L_ENC, D), target_grad.reshape(TABLES, TGT, D), totals[0], totals[1], totals[2], totals[3], totals[4], totals[5], totals[6])
```

```python
import jax
import jax.numpy as jnp
from jax import lax
from jax.sharding import PartitionSpec as P

HEAD = 64
SCALING = HEAD ** (-0.5)
EPSILON = 1e-05

bf16 = jnp.bfloat16
f32 = jnp.float32


def mm(a, b):
    return lax.dot_general(a, b, (((1,), (0,)), ((), ())), preferred_element_type=f32)


def mm_t(a, b):
    return lax.dot_general(a, b, (((1,), (1,)), ((), ())), preferred_element_type=f32)


def t_mm(a, b):
    return lax.dot_general(a, b, (((0,), (0,)), ((), ())), preferred_element_type=f32)


def norm_stats(summed):
    centered = summed - jnp.mean(summed, axis=-1, keepdims=True)
    spread = jnp.mean(centered * centered, axis=-1, keepdims=True)
    scale = lax.rsqrt(spread + EPSILON)
    return centered * scale, scale


def layer_norm(summed, gain, shift):
    return norm_stats(summed)[0] * gain + shift


def norm_backward(summed, gain, gradient):
    unit, scale = norm_stats(summed)
    scaled = gradient * gain
    inner = scaled - jnp.mean(scaled, axis=-1, keepdims=True)
    inner = inner - unit * jnp.mean(scaled * unit, axis=-1, keepdims=True)
    return (
        inner * scale,
        jnp.sum(gradient * unit, axis=0),
        jnp.sum(gradient, axis=0),
    )


def gelu_pair(before):
    cumulative = 0.5 * (1.0 + lax.erf(before * (0.5 ** 0.5)))
    density = jnp.exp(-0.5 * before * before) * 0.3989422804014327
    return before * cumulative, cumulative + before * density


def flip(value, bit):
    count = lax.axis_size("tensor")
    return lax.ppermute(value, "tensor", [(i, i ^ (1 << bit)) for i in range(count)])


def tensor_bits():
    return lax.axis_size("tensor").bit_length() - 1


def reduce_share(rows):
    bits = tensor_bits()
    for bit in range(bits):
        half = rows.shape[0] // 2
        sent = flip(rows[half:].astype(bf16), bit)
        rows = rows[:half].astype(f32) + sent.astype(f32)
    return rows


def gather_share(share):
    for bit in reversed(range(tensor_bits())):
        share = jnp.concatenate([share, flip(share, bit)], axis=0)
    return share


def reduce_half(rows):
    half = rows[0].astype(f32) + flip(rows[1].astype(bf16), 0).astype(f32)
    for bit in range(1, tensor_bits()):
        half = half.astype(bf16)
        half = half.astype(f32) + flip(half, bit).astype(f32)
    return half


def gather_half(half):
    return jnp.concatenate([half, flip(half, 0)], axis=0)


def to_second(value):
    return lax.ppermute(value, "section", [(0, 1)])


def to_first(value):
    return lax.ppermute(value, "section", [(1, 0)])


def split_heads(value):
    return value.reshape(value.shape[0], value.shape[1], -1, HEAD)


def attention_forward(queries, keys, values, allowed):
    scores = (
        jnp.einsum("gqhe,gkhe->ghqk", split_heads(queries), split_heads(keys), preferred_element_type=f32)
        * SCALING
    )
    scores = jnp.where(allowed[:, None], scores, -1e30)
    largest = jnp.max(scores, axis=-1, keepdims=True)
    exponent = jnp.exp(scores - largest)
    denominator = jnp.sum(exponent, axis=-1, keepdims=True)
    weights = (exponent / denominator).astype(bf16)
    output = jnp.einsum("ghqk,gkhe->gqhe", weights, split_heads(values), preferred_element_type=f32)
    return output.reshape(queries.shape), (largest + jnp.log(denominator))


def attention_backward(queries, keys, values, allowed, log_total, grads):
    q, k, v, g = map(split_heads, (queries, keys, values, grads))
    scores = jnp.einsum("gqhe,gkhe->ghqk", q, k, preferred_element_type=f32) * SCALING
    scores = jnp.where(allowed[:, None], scores, -1e30)
    probability = jnp.exp(scores - log_total)
    grad_value = jnp.einsum("ghqk,gqhe->gkhe", probability.astype(bf16), g, preferred_element_type=f32)
    grad_probs = jnp.einsum("gqhe,gkhe->ghqk", g, v, preferred_element_type=f32)
    inner = jnp.sum(probability * grad_probs, axis=-1, keepdims=True)
    grad_scores = (probability * (grad_probs - inner)).astype(bf16)
    grad_query = jnp.einsum("ghqk,gkhe->gqhe", grad_scores, k, preferred_element_type=f32) * SCALING
    grad_key = jnp.einsum("ghqk,gqhe->gkhe", grad_scores, q, preferred_element_type=f32) * SCALING
    return (
        grad_query.reshape(queries.shape).astype(bf16),
        grad_key.reshape(keys.shape).astype(bf16),
        grad_value.reshape(values.shape).astype(bf16),
    )


def per_device(
    table_input,
    target_input,
    cotangent,
    table_lengths,
    target_lengths,
    query_key,
    value_out,
    hidden_in,
    hidden_out,
    hidden_bias,
    vectors,
    cross_bias,
):
    sections = lax.axis_size("section")
    count = lax.axis_size("tensor")
    bits = tensor_bits()
    rank = lax.axis_index("tensor")
    section = lax.axis_index("section")
    is_first = section == 0
    tables, slots, width = table_input.shape
    targets = target_input.shape[1]
    columns = query_key.shape[3]
    rows = vectors[0]
    head_rows = lax.dynamic_slice_in_dim(rows[0:3], rank * columns, columns, 1)
    w_query, w_key, w_third_q = query_key[0, 0], query_key[0, 1], query_key[0, 2]
    w_value, w_out, w_third_v = value_out[0, 0], value_out[0, 1], value_out[0, 2]
    w_in, w_hidden_out, b_hidden = hidden_in[0], hidden_out[0], hidden_bias[0]
    w_cross_key, w_cross_value, b_cross_value = to_second(w_third_q), to_second(w_third_v), to_second(head_rows[2])

    masks = [int(format(p, f"0{bits}b")[::-1], 2) for p in range(count)]
    owners = rank ^ jnp.array(masks, jnp.int32)
    short = slots // (sections * count)
    row_index = (
        jnp.arange(sections)[None, :, None] * (count * short)
        + owners[:, None, None] * short
        + jnp.arange(short)[None, None, :]
    ).reshape(-1)
    table_rows = jnp.take(table_input.reshape(tables, sections, count, short, width), owners, axis=2)
    table_rows = jnp.swapaxes(table_rows, 1, 2).reshape(tables, slots, width)
    share = sections * short
    table_valid = row_index[None, :] < table_lengths[:, None]

    cores = 2
    small = targets // (sections * count)
    core_order = (rank % cores) ^ jnp.arange(cores)
    half = targets // cores

    def target_frame(value):
        split = value.reshape(tables, sections, count // cores, cores, small, width)
        split = jnp.take(split, core_order, axis=3)
        return jnp.transpose(split, (3, 0, 2, 1, 4, 5)).reshape(cores, tables * half, width)

    target_index = (
        jnp.arange(sections)[None, None, :, None] * (count * small)
        + jnp.arange(count // cores)[None, :, None, None] * (cores * small)
        + core_order[:, None, None, None] * small
        + jnp.arange(small)[None, None, None, :]
    ).reshape(-1)
    target_rows = target_frame(target_input)
    grad_rows_half = target_frame(cotangent)[0].astype(f32)
    target_valid = target_index[None, :] < target_lengths[:, None]
    causal = (target_index[None, :] <= target_index[:, None])[None] & target_valid[:, None, :]

    def per_table(value):
        return jnp.swapaxes(value.reshape(cores, tables, half, -1), 0, 1).reshape(tables, targets, -1)

    def in_frame(value):
        return jnp.swapaxes(value.reshape(tables, cores, half, -1), 0, 1).reshape(cores, tables * half, -1)

    def flat(value):
        return value.reshape(-1, value.shape[-1])

    def ffn_forward(inputs):
        hidden, slope = gelu_pair(mm(inputs, w_in) + b_hidden)
        hidden, slope = hidden.astype(bf16), slope.astype(bf16)
        return hidden, slope, mm_t(hidden, w_hidden_out).astype(bf16)

    def ffn_backward(grads, slope):
        grad_before = (mm(grads, w_hidden_out) * slope.astype(f32)).astype(bf16)
        return grad_before, mm_t(grad_before, w_in).astype(bf16)

    def encode(table):
        summed_zero = table_rows[table].astype(f32)
        normed = layer_norm(summed_zero, rows[9], rows[10])
        first_in = normed.astype(bf16)
        queries = (mm(first_in, w_query) + head_rows[0]).astype(bf16)
        keys = mm(first_in, w_key).astype(bf16)
        values = (mm(first_in, w_value) + head_rows[1]).astype(bf16)
        heads, log_total = attention_forward(queries[None], keys[None], values[None], table_valid[table][None, None])
        heads = heads[0].astype(bf16)
        summed_one = normed[:share] + reduce_share(mm_t(heads, w_out)) + rows[3]
        middle = layer_norm(summed_one, rows[5], rows[6])
        second_in = gather_share(middle.astype(bf16))
        hidden, slope, partial = ffn_forward(second_in)
        summed_two = middle + reduce_share(partial) + rows[4]
        memory = layer_norm(summed_two, rows[7], rows[8]).astype(bf16)
        kept = (summed_zero[:share], first_in, queries, keys, values, heads, log_total, summed_one, second_in, hidden, slope, summed_two)
        return memory, kept

    memories, kept_tables = zip(*[encode(table) for table in range(tables)])

    dec_first = flat(target_rows)
    dec_q = (mm(dec_first, w_query) + head_rows[0]).astype(bf16)
    dec_k = mm(dec_first, w_key).astype(bf16)
    dec_v = (mm(dec_first, w_value) + head_rows[1]).astype(bf16)
    dec_heads, dec_log = attention_forward(per_table(dec_q), per_table(dec_k), per_table(dec_v), causal)
    dec_heads = in_frame(dec_heads.astype(bf16))
    dec_one = (
        target_rows[0].astype(f32)
        + reduce_half(mm_t(flat(dec_heads), w_out).reshape(cores, -1, width))
        + rows[3]
    )
    dec_middle = layer_norm(dec_one, rows[5], rows[6])
    cross_in = gather_half(dec_middle.astype(bf16))
    cross_q = (mm(cross_in, w_third_q) + head_rows[2]).astype(bf16)

    memory_rows = jnp.stack([gather_share(to_second(memory)) for memory in memories])
    cross_k = mm(flat(memory_rows), w_cross_key).astype(bf16).reshape(tables, slots, columns)
    cross_v = (mm(flat(memory_rows), w_cross_value) + b_cross_value).astype(bf16).reshape(tables, slots, columns)
    cross_heads, cross_log = attention_forward(per_table(cross_q), cross_k, cross_v, table_valid[:, None])
    cross_heads = flat(in_frame(cross_heads.astype(bf16)))
    dec_three = dec_middle + reduce_half(mm_t(cross_heads, w_third_v).reshape(cores, -1, width)) + cross_bias
    dec_later = layer_norm(dec_three, rows[9], rows[10])
    third_in = gather_half(dec_later.astype(bf16))
    dec_hidden, dec_slope, partial = ffn_forward(third_in)
    dec_two = dec_later + reduce_half(partial.reshape(cores, -1, width)) + rows[4]
    decoded = layer_norm(dec_two, rows[7], rows[8]).astype(bf16)

    grad_two, dec_gain_two, dec_shift_two = norm_backward(dec_two, rows[7], grad_rows_half)
    grad_two_rows = gather_half(grad_two.astype(bf16))
    dec_before_grad, partial = ffn_backward(grad_two_rows, dec_slope)
    grad_later = reduce_half(partial.reshape(cores, -1, width))
    grad_three, dec_gain_three, dec_shift_three = norm_backward(dec_three, rows[9], grad_two + grad_later)
    grad_three_rows = gather_half(grad_three.astype(bf16))
    grad_cross_heads = mm(grad_three_rows, w_third_v).astype(bf16)
    grad_cross_q, grad_cross_k, grad_cross_v = attention_backward(
        per_table(cross_q), cross_k, cross_v, table_valid[:, None], cross_log, per_table(grad_cross_heads)
    )
    grad_memory = []
    for table in range(tables):
        partial = mm_t(grad_cross_k[table], w_cross_key) + mm_t(grad_cross_v[table], w_cross_value)
        grad_memory.append(to_first(reduce_share(partial).astype(bf16)).astype(f32))
    third_q_grad = to_first(t_mm(flat(memory_rows), flat(grad_cross_k)).astype(bf16))
    third_v_grad = to_first(t_mm(flat(memory_rows), flat(grad_cross_v)).astype(bf16))
    third_bias_grad = to_first(jnp.sum(flat(grad_cross_v).astype(f32), axis=0))

    grad_cross_q = flat(in_frame(grad_cross_q))
    grad_middle = reduce_half(mm_t(grad_cross_q, w_third_q).reshape(cores, -1, width))
    grad_one, dec_gain_one, dec_shift_one = norm_backward(dec_one, rows[5], grad_three + grad_middle)
    grad_one_rows = gather_half(grad_one.astype(bf16))
    grad_heads = mm(grad_one_rows, w_out).astype(bf16)
    grad_q, grad_k, grad_v = attention_backward(
        per_table(dec_q), per_table(dec_k), per_table(dec_v), causal, dec_log, per_table(grad_heads)
    )
    grad_q, grad_k, grad_v = (flat(in_frame(value)) for value in (grad_q, grad_k, grad_v))
    partial = mm_t(grad_q, w_query) + mm_t(grad_k, w_key) + mm_t(grad_v, w_value)
    target_grad = (grad_one + reduce_half(partial.reshape(cores, -1, width))).astype(bf16)
    dec_matrix = (
        t_mm(dec_first, grad_q),
        t_mm(dec_first, grad_k),
        t_mm(cross_in, grad_cross_q),
        t_mm(dec_first, grad_v),
        t_mm(grad_one_rows, flat(dec_heads)),
        t_mm(grad_three_rows, cross_heads),
        t_mm(third_in, dec_before_grad),
        t_mm(grad_two_rows, dec_hidden),
    )
    dec_head_rows = [jnp.sum(value.astype(f32), axis=0) for value in (grad_q, grad_v, grad_cross_q)]
    dec_bias = jnp.sum(dec_before_grad.astype(f32), axis=0)
    doubled = cores / count
    dec_rows = [
        value * doubled
        for value in (
            jnp.sum(grad_one, axis=0),
            jnp.sum(grad_two, axis=0),
            dec_gain_one,
            dec_shift_one,
            dec_gain_two,
            dec_shift_two,
            dec_gain_three,
            dec_shift_three,
            jnp.sum(grad_three, axis=0),
        )
    ]

    def encode_back(table):
        (summed_zero, first_in, queries, keys, values, heads, log_total, summed_one, second_in, hidden, slope, summed_two) = (
            kept_tables[table]
        )
        grad_two, gain_two, shift_two = norm_backward(summed_two, rows[7], grad_memory[table])
        grad_two_rows = gather_share(grad_two.astype(bf16))
        grad_before, partial = ffn_backward(grad_two_rows, slope)
        grad_middle = reduce_share(partial)
        grad_one, gain_one, shift_one = norm_backward(summed_one, rows[5], grad_two + grad_middle)
        grad_one_rows = gather_share(grad_one.astype(bf16))
        grad_heads = mm(grad_one_rows, w_out).astype(bf16)
        grad_q, grad_k, grad_v = (
            value[0]
            for value in attention_backward(
                queries[None], keys[None], values[None], table_valid[table][None, None], log_total, grad_heads[None]
            )
        )
        partial = mm_t(grad_q, w_query) + mm_t(grad_k, w_key) + mm_t(grad_v, w_value)
        grad_normed = reduce_share(partial)
        table_grad, gain_zero, shift_zero = norm_backward(summed_zero, rows[9], grad_one + grad_normed)
        sums = (
            jnp.sum(grad_one, axis=0),
            jnp.sum(grad_two, axis=0),
            gain_one,
            shift_one,
            gain_two,
            shift_two,
            gain_zero,
            shift_zero,
        )
        pairs = (first_in, grad_q, grad_k, grad_v, grad_one_rows, heads, second_in, grad_before, grad_two_rows, hidden)
        return table_grad.astype(bf16), sums, pairs

    table_grads, sums, pairs = zip(*[encode_back(table) for table in range(tables)])
    enc_rows = [sum(values) for values in zip(*sums)]
    (first_in, grad_q, grad_k, grad_v, grad_one_rows, heads, second_in, grad_before, grad_two_rows, hidden) = (
        jnp.concatenate(values) for values in zip(*pairs)
    )
    enc_matrix = (
        t_mm(first_in, grad_q),
        t_mm(first_in, grad_k),
        third_q_grad,
        t_mm(first_in, grad_v),
        t_mm(grad_one_rows, heads),
        third_v_grad,
        t_mm(second_in, grad_before),
        t_mm(grad_two_rows, hidden),
    )
    enc_head_rows = [jnp.sum(grad_q.astype(f32), axis=0), jnp.sum(grad_v.astype(f32), axis=0), third_bias_grad]
    enc_bias = jnp.sum(grad_before.astype(f32), axis=0)

    matrix = [
        lax.psum(jnp.where(is_first, own.astype(bf16), other.astype(bf16)), "dp").astype(f32)
        for own, other in zip(enc_matrix, dec_matrix)
    ]
    query_key_grad = jnp.stack(matrix[0:3])
    value_out_grad = jnp.stack(matrix[3:6])

    head_sums = jnp.where(is_first, jnp.stack(enc_head_rows), jnp.stack(dec_head_rows))
    placed = lax.dynamic_update_slice(jnp.zeros((3, width), f32), head_sums, (0, rank * columns))
    other_rows = jnp.where(is_first, jnp.stack(enc_rows), jnp.stack(dec_rows[:8]))
    cross_row = jnp.where(is_first, 0.0, dec_rows[8])
    bias_sum = lax.psum(jnp.where(is_first, enc_bias, dec_bias), "dp")
    vector_total = lax.psum(jnp.concatenate([placed, other_rows]), ("dp", "tensor"))
    cross_total = lax.psum(cross_row, ("section", "dp", "tensor"))

    table_grads = jnp.stack(table_grads).reshape(tables, sections, short, width)
    moved_up = lax.ppermute(table_grads[:, 1], "section", [(0, 1)])
    table_out = jnp.where(is_first, table_grads[:, 0], moved_up)
    own = lax.dynamic_slice_in_dim(
        jnp.stack([decoded, target_grad]).reshape(2, tables, count // cores, sections, small, width),
        rank // cores,
        1,
        2,
    )[:, :, 0]
    moved_down = lax.ppermute(own[:, :, 0], "section", [(1, 0)])
    small_out = jnp.where(is_first, moved_down, own[:, :, 1])
    return (
        small_out[0],
        table_out,
        small_out[1],
        query_key_grad[None],
        value_out_grad[None],
        matrix[6][None],
        matrix[7][None],
        bias_sum[None],
        vector_total[None],
        cross_total,
    )


def solution(mesh):
    in_specs = (
        P("dp", None, None),
        P("dp", None, None),
        P("dp", None, None),
        P("dp"),
        P("dp"),
        P("section", None, None, "tensor"),
        P("section", None, None, "tensor"),
        P("section", None, "tensor"),
        P("section", None, "tensor"),
        P("section", "tensor"),
        P("section", None, None),
        P(),
    )
    out_specs = (
        P("dp", ("section", "tensor"), None),
        P("dp", ("section", "tensor"), None),
        P("dp", ("section", "tensor"), None),
        P("section", None, None, "tensor"),
        P("section", None, None, "tensor"),
        P("section", None, "tensor"),
        P("section", None, "tensor"),
        P("section", "tensor"),
        P("section", None, None),
        P(),
    )
    return jax.shard_map(
        per_device, mesh=mesh, in_specs=in_specs, out_specs=out_specs, check_vma=False
    )
```

```python
import jax
import jax.numpy as jnp
from jax import lax
from jax.experimental import pallas as pl
from jax.experimental.pallas import tpu as pltpu
from jax.sharding import PartitionSpec as P

HEAD = 64
SCALING = HEAD ** (-0.5)
EPSILON = 1e-05

bf16 = jnp.bfloat16
f32 = jnp.float32


def mm(a, b):
    return lax.dot_general(a, b, (((1,), (0,)), ((), ())), preferred_element_type=f32)


def mm_t(a, b):
    return lax.dot_general(a, b, (((1,), (1,)), ((), ())), preferred_element_type=f32)


def t_mm(a, b):
    return lax.dot_general(a, b, (((0,), (0,)), ((), ())), preferred_element_type=f32)


def norm_stats(summed):
    centered = summed - jnp.mean(summed, axis=-1, keepdims=True)
    spread = jnp.mean(centered * centered, axis=-1, keepdims=True)
    scale = lax.rsqrt(spread + EPSILON)
    return centered * scale, scale


def gelu_pair(before):
    cumulative = 0.5 * (1.0 + lax.erf(before * (0.5 ** 0.5)))
    density = jnp.exp(-0.5 * before * before) * 0.3989422804014327
    return before * cumulative, cumulative + before * density


def shaped(rows, width, dtype=bf16):
    return jax.ShapeDtypeStruct((rows, width), dtype)


def full(shape):
    return pl.BlockSpec(shape, lambda *_: (0,) * len(shape))


def turned(steps):
    return lambda i, *_: ((i + steps // 2) % steps, 0)


def low_high(rows, width, steps):
    return [
        pl.BlockSpec((rows, width), lambda i, *_: (jnp.maximum(i - steps // 2, 0), 0)),
        pl.BlockSpec((rows, width), lambda i, *_: (jnp.minimum(i, steps // 2 - 1), 0)),
    ]


def put_low_high(value, low, high):
    first = pl.program_id(0) < pl.num_programs(0) // 2

    @pl.when(first)
    def _():
        high[...] = value

    @pl.when(jnp.logical_not(first))
    def _():
        low[...] = value


def pick_block(parts, held):
    steps = len(parts)
    at = (pl.program_id(0) + steps // 2) % steps
    for index, part in enumerate(parts):
        @pl.when(at == index)
        def _(part=part):
            held[...] = part[...]
    return held[...]


def cost(flops, moved, exps=0):
    return pl.CostEstimate(flops=int(flops), bytes_accessed=int(moved), transcendentals=int(exps))


class Order:
    def __init__(self):
        self.last = None


order = Order()


def call(kernel, grid, in_specs, out_specs, out_shape, scratch, estimate, *args, prefetch=()):
    count = len(prefetch) + len(args)
    after = [] if order.last is None else [order.last]

    def ordered(*refs):
        kernel(*refs[:count], *refs[count + len(after) :])

    grid_spec = pltpu.PrefetchScalarGridSpec(
        num_scalar_prefetch=len(prefetch),
        grid=grid,
        in_specs=list(in_specs) + [pl.BlockSpec(memory_space=pl.ANY)] * len(after),
        out_specs=out_specs,
        scratch_shapes=scratch,
    )
    results = pl.pallas_call(
        ordered,
        grid_spec=grid_spec,
        out_shape=out_shape,
        compiler_params=pltpu.CompilerParams(vmem_limit_bytes=48 * 1024 * 1024),
        cost_estimate=estimate,
        name=kernel.__qualname__.split(".")[0],
    )(*prefetch, *args, *after)
    order.last = min(results, key=lambda result: result.size) if isinstance(results, (list, tuple)) else results
    return results


def gate(*values, behind=()):
    count = len(values)
    after = ([] if order.last is None else [order.last]) + list(behind)
    results = pl.pallas_call(
        lambda *refs: None,
        in_specs=[pl.BlockSpec(memory_space=pl.ANY)] * (count + len(after)),
        out_specs=[pl.BlockSpec(memory_space=pl.ANY)] * count,
        out_shape=[jax.ShapeDtypeStruct(value.shape, value.dtype) for value in values],
        input_output_aliases={index: index for index in range(count)},
        cost_estimate=cost(0, 0),
        name="gate",
    )(*values, *after)
    order.last = results[0]
    return results if count > 1 else results[0]


def norm_kernel(residual, keep, sent, bias, gain, shift, summed_out, wide_out, out):
    summed = residual[...] + (keep[...].astype(f32) + sent[...].astype(f32)) + bias[...]
    normed = norm_stats(summed)[0] * gain[...] + shift[...]
    summed_out[...] = summed
    wide_out[...] = normed
    out[...] = normed.astype(bf16)


def norm_forward(residual, parts, bias, gain, shift):
    rows, width = residual.shape
    block, row = full((rows, width)), full((1, width))
    return call(
        norm_kernel, (1,), [block] * 3 + [row] * 3, [block] * 3,
        [shaped(rows, width, f32)] * 2 + [shaped(rows, width)], [],
        cost(12 * rows * width, 18 * rows * width),
        residual, *parts, bias, gain, shift,
    )


def norm_back_kernel(count, *refs):
    grads, (summed, gain, wide_out, out, sums) = refs[:count], refs[count:]
    gradient = grads[0][...].astype(f32)
    for grad in grads[1:]:
        gradient = gradient + grad[...].astype(f32)
    unit, scale = norm_stats(summed[...].astype(f32))
    scaled = gradient * gain[...]
    inner = scaled - jnp.mean(scaled, axis=-1, keepdims=True)
    inner = (inner - unit * jnp.mean(scaled * unit, axis=-1, keepdims=True)) * scale
    wide_out[...] = inner
    out[...] = inner.astype(bf16)
    sums[...] = jnp.concatenate(
        [
            jnp.sum(gradient * unit, axis=0, keepdims=True),
            jnp.sum(gradient, axis=0, keepdims=True),
            jnp.sum(inner, axis=0, keepdims=True),
            jnp.zeros((5, inner.shape[1]), f32),
        ]
    )


def norm_backward(summed, gain, grads):
    rows, width = summed.shape
    block, row = full((rows, width)), full((1, width))

    def kernel(*refs):
        norm_back_kernel(len(grads), *refs)

    return call(
        kernel, (1,), [block] * (len(grads) + 1) + [row], [block] * 2 + [full((8, width))],
        [shaped(rows, width, f32), shaped(rows, width), shaped(8, width, f32)], [],
        cost(20 * rows * width, 18 * rows * width),
        *grads, summed, gain,
    )


def qkv_kernel(sections, owners, *refs):
    parts = refs[:sections]
    gain, shift, w_q, w_k, w_v, bias, x_out, q_out, k_out, v_out, own_norm, own_raw = refs[sections:]
    raw = jnp.concatenate([part[...] for part in parts], axis=0)
    normed = norm_stats(raw.astype(f32))[0] * gain[...] + shift[...]
    x = normed.astype(bf16)
    x_out[...] = x
    q_out[...] = (mm(x, w_q[...]) + bias[0:1]).astype(bf16)
    k_out[...] = mm(x, w_k[...]).astype(bf16)
    v_out[...] = (mm(x, w_v[...]) + bias[1:2]).astype(bf16)

    @pl.when(pl.program_id(0) == 0)
    def _():
        own_norm[...] = normed
        own_raw[...] = raw


def encoder_qkv(table_rows, table, owners, gain, shift, w_q, w_k, w_v, bias, sections):
    slots, width = table_rows.shape[1:]
    count = owners.shape[0]
    short = slots // (sections * count)
    share = sections * short
    columns = w_q.shape[1]

    def part_spec(s):
        return pl.BlockSpec((None, short, width), lambda i, order: (table, s * count + order[i], 0))

    def block(columns):
        return pl.BlockSpec((share, columns), lambda i, order: (i, 0))

    def kernel(*refs):
        qkv_kernel(sections, *refs)

    return call(
        kernel, (count,),
        [part_spec(s) for s in range(sections)] + [full((1, width))] * 2 + [full((width, columns))] * 3 + [full(bias.shape)],
        [block(width)] + [block(columns)] * 3 + [full((share, width))] * 2,
        [shaped(slots, width)] + [shaped(slots, columns)] * 3 + [shaped(share, width, f32), shaped(share, width)],
        [],
        cost(6 * slots * width * columns, 8 * slots * width),
        *([table_rows] * sections), gain, shift, w_q, w_k, w_v, bias,
        prefetch=[owners],
    )


def pair_mask(head):
    return (lax.broadcasted_iota(jnp.int32, (1, 128), 1) // HEAD) == head


def attention_rows(q_all, k_all, v_all, mask):
    rows, columns = q_all.shape
    lanes = lax.broadcasted_iota(jnp.int32, (rows, 128), 1)
    logs = jnp.zeros((rows, 128), f32)
    parts = []
    for pair in range(columns // 128):
        at = slice(pair * 128, pair * 128 + 128)
        q = q_all[:, at] * jnp.asarray(SCALING, bf16)
        k, v = k_all[:, at], v_all[:, at]
        outs = []
        for head in range(2):
            scores = mm_t(jnp.where(pair_mask(head), q, jnp.zeros_like(q)), k) + mask
            largest = jnp.max(scores, axis=-1, keepdims=True)
            exponent = jnp.exp(scores - largest)
            total = jnp.sum(exponent, axis=-1, keepdims=True)
            outs.append(mm(exponent.astype(bf16), v) / total)
            logs = jnp.where(lanes == pair * 2 + head, largest + jnp.log(total), logs)
        parts.append(jnp.where(pair_mask(0), outs[0], outs[1]))
    return jnp.concatenate(parts, axis=1), jnp.transpose(logs)


def attention_kernel(q_ref, k_ref, v_ref, mask_ref, w_out, heads_out, wide_out, log_out, low, high):
    wide, logs = attention_rows(q_ref[...], k_ref, v_ref, mask_ref[...])
    heads = wide.astype(bf16)
    wide_out[...] = wide
    heads_out[...] = heads
    log_out[...] = logs[: log_out.shape[0]]
    put_low_high(mm_t(heads, w_out[...]).astype(bf16), low, high)


def encoder_attention(queries, keys, values, mask, w_out, steps):
    slots, columns = queries.shape
    width = w_out.shape[0]
    rows = slots // steps
    block = pl.BlockSpec((rows, columns), turned(steps))
    return call(
        attention_kernel, (steps,),
        [block, full((slots, columns)), full((slots, columns)), full((1, slots)), full((width, columns))],
        [block, block, pl.BlockSpec((8, rows), lambda i: (0, (i + steps // 2) % steps))] + low_high(rows, width, steps),
        [shaped(slots, columns), shaped(slots, columns, f32), shaped(8, slots, f32)] + [shaped(slots // 2, width)] * 2,
        [],
        cost(8 * slots * slots * columns, 8 * slots * columns + 2 * slots * width, slots * slots * columns // HEAD),
        queries, keys, values, mask, w_out,
    )


def attention_back_rows(grads, wide, logs, q_all, k_all, v_all, mask, add):
    inner = jnp.transpose(grads.astype(f32) * wide)
    sub = lax.broadcasted_iota(jnp.int32, (128, 1), 0) // HEAD
    parts = []
    for pair in range(grads.shape[1] // 128):
        at = slice(pair * 128, pair * 128 + 128)
        q = q_all[:, at] * jnp.asarray(SCALING, bf16)
        k, v, g = k_all[:, at], v_all[:, at], grads[:, at]
        dk, dv, dq = 0.0, 0.0, []
        for head in range(2):
            keep = pair_mask(head)
            q_one = jnp.where(keep, q, jnp.zeros_like(q))
            g_one = jnp.where(keep, g, jnp.zeros_like(g))
            at_head = pair * 2 + head
            probability = jnp.exp((mm_t(k, q_one) + mask) - logs[at_head : at_head + 1, :])
            dv = dv + mm(probability.astype(bf16), g_one)
            delta = jnp.sum(inner[at_head * HEAD : (at_head + 1) * HEAD], axis=0, keepdims=True)
            scores_grad = (probability * (mm_t(v, g_one) - delta)).astype(bf16)
            dk = dk + mm(scores_grad, q_one)
            dq.append(t_mm(k, scores_grad))
        add(at, dk, dv)
        parts.append(jnp.transpose(jnp.where(sub == 0, dq[0], dq[1]) * SCALING))
    return jnp.concatenate(parts, axis=1).astype(bf16)


def attention_back_kernel(steps, *refs):
    parts = refs[:steps]
    (wide_ref, log_ref, q_ref, k_ref, v_ref, mask_ref, w_out, rows_out, dq_out, dk_out, dv_out, q_sum, v_sum, held, dk_sum, dv_sum) = refs[steps:]
    step = pl.program_id(0)
    grad_rows = pick_block(parts, held)
    rows_out[...] = grad_rows
    grads = mm(grad_rows, w_out[...]).astype(bf16)

    @pl.when(step == 0)
    def _():
        dk_sum[...] = jnp.zeros_like(dk_sum)
        dv_sum[...] = jnp.zeros_like(dv_sum)
        q_sum[...] = jnp.zeros_like(q_sum)

    def add(at, dk, dv):
        dk_sum[:, at] += dk
        dv_sum[:, at] += dv

    dq = attention_back_rows(grads, wide_ref[...], log_ref, q_ref[...], k_ref, v_ref, mask_ref[...], add)
    dq_out[...] = dq
    q_sum[...] += jnp.sum(dq.astype(f32), axis=0, keepdims=True)

    @pl.when(step == steps - 1)
    def _():
        dk_out[...] = dk_sum[...].astype(bf16)
        dv = dv_sum[...].astype(bf16)
        dv_out[...] = dv
        v_sum[...] = jnp.sum(dv.astype(f32), axis=0, keepdims=True)


def encoder_attention_back(grad_parts, wide, logs, queries, keys, values, mask, w_out):
    slots, columns = queries.shape
    width = w_out.shape[0]
    steps = len(grad_parts)
    rows = slots // steps
    whole, row = full((slots, columns)), full((1, columns))
    block = pl.BlockSpec((rows, columns), turned(steps))

    def kernel(*refs):
        attention_back_kernel(steps, *refs)

    return call(
        kernel, (steps,),
        [full((rows, width))] * steps
        + [block, pl.BlockSpec((8, rows), lambda i: (0, (i + steps // 2) % steps)), block, whole, whole, full((slots, 1)), full((width, columns))],
        [pl.BlockSpec((rows, width), turned(steps)), block, whole, whole, row, row],
        [shaped(slots, width)] + [shaped(slots, columns)] * 3 + [shaped(1, columns, f32)] * 2,
        [pltpu.VMEM((rows, width), bf16)] + [pltpu.VMEM((slots, columns), f32)] * 2,
        cost(20 * slots * slots * columns, 16 * slots * columns + 2 * slots * width, slots * slots * columns // HEAD),
        *grad_parts, wide, logs, queries, keys, values, mask, w_out,
    )


def ffn_kernel(steps, *refs):
    parts, (w_in, bias, w_out, x_out, hidden_out, slope_out, low, high, held) = refs[:steps], refs[steps:]
    x = pick_block(parts, held)
    x_out[...] = x
    hidden, slope = gelu_pair(mm(x, w_in[...]) + bias[...])
    hidden = hidden.astype(bf16)
    hidden_out[...] = hidden
    slope_out[...] = slope.astype(bf16)
    put_low_high(mm_t(hidden, w_out[...]).astype(bf16), low, high)


def ffn_forward(parts, w_in, bias, w_out):
    steps = len(parts)
    rows, width = parts[0].shape
    slots = rows * steps
    units = w_in.shape[1]
    block = pl.BlockSpec((rows, units), turned(steps))

    def kernel(*refs):
        ffn_kernel(steps, *refs)

    return call(
        kernel, (steps,),
        [full((rows, width))] * steps + [full((width, units)), full((1, units)), full((width, units))],
        [pl.BlockSpec((rows, width), turned(steps)), block, block] + low_high(rows, width, steps),
        [shaped(slots, width)] + [shaped(slots, units)] * 2 + [shaped(slots // 2, width)] * 2,
        [pltpu.VMEM((rows, width), bf16)],
        cost(4 * slots * width * units, 8 * slots * units + 4 * units * width, 2 * slots * units),
        *parts, w_in, bias, w_out,
    )


def ffn_back_kernel(steps, *refs):
    parts, (slope, w_in, w_out, x_out, before_out, low, high, bias_out, held) = refs[:steps], refs[steps:]
    x = pick_block(parts, held)
    x_out[...] = x
    before = (mm(x, w_out[...]) * slope[...].astype(f32)).astype(bf16)
    before_out[...] = before

    @pl.when(pl.program_id(0) == 0)
    def _():
        bias_out[...] = jnp.zeros_like(bias_out)

    bias_out[...] += jnp.sum(before.astype(f32), axis=0, keepdims=True)
    put_low_high(mm_t(before, w_in[...]).astype(bf16), low, high)


def ffn_backward(parts, slope, w_in, w_out):
    steps = len(parts)
    rows, width = parts[0].shape
    slots = rows * steps
    units = w_in.shape[1]
    block = pl.BlockSpec((rows, units), turned(steps))

    def kernel(*refs):
        ffn_back_kernel(steps, *refs)

    return call(
        kernel, (steps,),
        [full((rows, width))] * steps + [block, full((width, units)), full((width, units))],
        [pl.BlockSpec((rows, width), turned(steps)), block] + low_high(rows, width, steps) + [full((1, units))],
        [shaped(slots, width), shaped(slots, units)] + [shaped(slots // 2, width)] * 2 + [shaped(1, units, f32)],
        [pltpu.VMEM((rows, width), bf16)],
        cost(4 * slots * width * units, 6 * slots * units + 4 * units * width),
        *parts, slope, w_in, w_out,
    )


def back_sum(values, matrices, steps):
    slots, columns = values[0].shape
    width = matrices[0].shape[0]
    rows = slots // steps
    count = len(values)

    def kernel(*refs):
        total = 0.0
        for value, matrix in zip(refs[:count], refs[count : 2 * count]):
            total = total + mm_t(value[...], matrix[...])
        put_low_high(total.astype(bf16), *refs[2 * count :])

    return call(
        kernel, (steps,),
        [pl.BlockSpec((rows, columns), turned(steps))] * count + [full((width, columns))] * count,
        low_high(rows, width, steps),
        [shaped(slots // 2, width)] * 2, [],
        cost(2 * count * slots * width * columns, 2 * slots * width),
        *values, *matrices,
    )


def project_parts(parts, matrices, biases):
    steps = len(parts)
    rows, width = parts[0].shape
    slots = rows * steps
    columns = matrices[0].shape[1]
    count = len(matrices)

    def kernel(*refs):
        held = refs[-1]
        x = pick_block(refs[:steps], held)
        inner = refs[steps:-1]
        inner[2 * count][...] = x
        for index in range(count):
            inner[2 * count + 1 + index][...] = (mm(x, inner[index][...]) + inner[count + index][...]).astype(bf16)

    return call(
        kernel, (steps,),
        [full((rows, width))] * steps + [full((width, columns))] * count + [full((1, columns))] * count,
        [pl.BlockSpec((rows, width), turned(steps))] + [pl.BlockSpec((rows, columns), turned(steps))] * count,
        [shaped(slots, width)] + [shaped(slots, columns)] * count,
        [pltpu.VMEM((rows, width), bf16)],
        cost(2 * count * slots * width * columns, 4 * slots * width),
        *parts, *matrices, *biases,
    )


CHUNKS = 4


MASKS = (0, 2, 1, 3)


def weight_grad(section, order_ref, enc_pairs, dec_pairs):
    width = dec_pairs[0][0].shape[1]
    chunk = width // CHUNKS
    tables, count = len(enc_pairs), len(dec_pairs)
    total_columns = sum(g.shape[1] for _, g in dec_pairs)
    flat = [pair for pairs in (*enc_pairs, dec_pairs) for pair in pairs]

    def kernel(at, order_at, *refs):
        ins, (low, high) = refs[: 2 * len(flat)], refs[2 * len(flat) :]

        def product(index):
            return jnp.concatenate(
                [t_mm(ins[2 * (index * count + one)][...], ins[2 * (index * count + one) + 1][...]) for one in range(count)], axis=1
            )

        @pl.when(at[0] == 0)
        def _():
            total = 0.0
            for table in range(tables):
                total = total + product(table)
            put_low_high(total.astype(bf16), low, high)

        @pl.when(at[0] != 0)
        def _():
            put_low_high(product(tables).astype(bf16), low, high)

    in_specs, args = [], []
    for x, g in flat:
        in_specs += [pl.BlockSpec((x.shape[0], chunk), lambda i, s, at: (0, at[i])), full(g.shape)]
        args += [x, g]
    rows = sum(x.shape[0] for x, _ in flat) // count
    half = jax.ShapeDtypeStruct((2, chunk, total_columns), bf16)
    return call(
        kernel, (CHUNKS,), in_specs,
        [
            pl.BlockSpec((None, chunk, total_columns), lambda i, *_: (jnp.maximum(i - 2, 0), 0, 0)),
            pl.BlockSpec((None, chunk, total_columns), lambda i, *_: (jnp.minimum(i, 1), 0, 0)),
        ],
        [half] * 2, [],
        cost(2 * rows * width * total_columns, 2 * rows * (width + total_columns)),
        *args,
        prefetch=[section, order_ref],
    )


def sum_places(low, high, parts):
    chunk, columns = low.shape[1:]
    if lax.axis_size("dp") != CHUNKS:
        low, high = lax.psum((low, high), "dp")
        parts.extend([low[0], low[1], high[0], high[1]])
        return
    sent = flip(high, 0, "dp")
    yield "made"

    def add_pair(low_ref, sent_ref, own, far):
        own[...] = (low_ref[0].astype(f32) + sent_ref[0].astype(f32)).astype(bf16)
        far[...] = (low_ref[1].astype(f32) + sent_ref[1].astype(f32)).astype(bf16)

    whole = pl.BlockSpec(low.shape, lambda *_: (0, 0, 0))
    own, far = call(
        add_pair, (1,), [whole] * 2, [full((chunk, columns))] * 2, [shaped(chunk, columns)] * 2, [], cost(0, 6 * low.size), low, sent
    )
    sent = flip(far, 1, "dp")
    yield "one"
    total = add_rows(own, sent)
    second = flip(total, 1, "dp")
    third = flip(total, 0, "dp")
    yield "two"
    second = gate(second)
    fourth = flip(second, 0, "dp")
    parts.extend([total, second, third, fourth])
    yield "three"


def put_chunk(place, parts, put):
    other = place[0] ^ pl.program_id(0)
    for part, mask in zip(parts, MASKS):
        @pl.when(other == mask)
        def _(part=part):
            put(part)


def unite_one(place, parts):
    chunk, columns = parts[0].shape

    def kernel(place_at, *refs):
        def put(part):
            refs[-1][...] = part[...].astype(f32)

        put_chunk(place_at, refs[:-1], put)

    return call(
        kernel, (CHUNKS,), [full((chunk, columns))] * CHUNKS, pl.BlockSpec((chunk, columns), lambda i, *_: (i, 0)),
        shaped(CHUNKS * chunk, columns, f32), [], cost(0, 24 * chunk * columns), *parts,
        prefetch=[place],
    )


def pick_third(section, place, arrived, own):
    width, columns = own[0].shape
    rows = width // CHUNKS

    def kernel(at, place_at, *refs):
        turn = (pl.program_id(0) - place_at[0]) % CHUNKS
        first = at[0] == 0
        value = jnp.concatenate([jnp.where(first, a[...], b[...]) for a, b in zip(refs[:2], refs[2:4])], axis=1)
        for index in range(CHUNKS):
            @pl.when(turn == index)
            def _(index=index):
                refs[4 + index][...] = value

    block = pl.BlockSpec((rows, columns), lambda i, *_: (i, 0))
    return call(
        kernel, (CHUNKS,), [block] * 4, [full((rows, 2 * columns))] * CHUNKS, [shaped(rows, 2 * columns)] * CHUNKS, [],
        cost(0, 8 * width * columns), *arrived, *own,
        prefetch=[section, place],
    )


def send_chunks(chunks):
    return [lax.ppermute(chunk, "dp", [(i, (i + s + 1) % CHUNKS) for i in range(CHUNKS)]) for s, chunk in enumerate(chunks)]


def sum_chunks(own, sent):
    def kernel(*refs):
        total = refs[0][...].astype(f32)
        for ref in refs[1:-1]:
            total = total + ref[...].astype(f32)
        refs[-1][...] = total.astype(bf16)

    return call(
        kernel, (1,), [full(own.shape)] * CHUNKS, full(own.shape), shaped(*own.shape), [], cost(0, 10 * own.size), own, *sent
    )


def unite(place, qk, vo, thirds):
    rows, columns = qk[0].shape[0], qk[0].shape[1] // 2

    def kernel(place_at, *refs):
        qk, vo, chunks, (first, second) = refs[:CHUNKS], refs[CHUNKS : 2 * CHUNKS], refs[2 * CHUNKS : 3 * CHUNKS], refs[3 * CHUNKS :]
        for parts, out in ((qk, first), (vo, second)):
            def put(part, out=out):
                out[0] = part[:, :columns].astype(f32)
                out[1] = part[:, columns:].astype(f32)

            put_chunk(place_at, parts, put)
        turn = (place_at[0] - pl.program_id(0)) % CHUNKS
        for index in range(CHUNKS):
            @pl.when(turn == index)
            def _(index=index):
                first[2] = chunks[index][:, :columns].astype(f32)
                second[2] = chunks[index][:, columns:].astype(f32)

    stacked = pl.BlockSpec((3, rows, columns), lambda i, *_: (0, i, 0))
    return call(
        kernel, (CHUNKS,), [full((rows, 2 * columns))] * (3 * CHUNKS), [stacked] * 2,
        [jax.ShapeDtypeStruct((3, CHUNKS * rows, columns), f32)] * 2, [],
        cost(0, 36 * CHUNKS * rows * columns), *qk, *vo, *thirds,
        prefetch=[place],
    )


def weight_sum(xs, gs):
    count = len(xs)
    width, columns = xs[0].shape[1], gs[0].shape[1]

    def kernel(*refs):
        total = t_mm(refs[0][...], refs[count][...])
        for index in range(1, count):
            total = total + t_mm(refs[index][...], refs[count + index][...])
        refs[-1][...] = total.astype(bf16)

    rows = sum(x.shape[0] for x in xs)
    return call(
        kernel, (1,), [full(value.shape) for value in (*xs, *gs)], full((width, columns)), shaped(width, columns), [],
        cost(2 * rows * width * columns, 2 * rows * (width + columns)),
        *xs, *gs,
    )


def add_halves(low, sent):
    rows, width = low.shape[0] // 2, low.shape[1]

    def kernel(low_ref, sent_ref, low_out, high_out):
        total = (low_ref[...].astype(f32) + sent_ref[...].astype(f32)).astype(bf16)
        low_out[...] = total[:rows]
        high_out[...] = total[rows:]

    return call(
        kernel, (1,), [full((2 * rows, width))] * 2, [full((rows, width))] * 2, [shaped(rows, width)] * 2, [],
        cost(2 * rows * width, 12 * rows * width), low, sent,
    )


def add_rows(low, sent):
    rows, width = low.shape

    def kernel(low_ref, sent_ref, out):
        out[...] = (low_ref[...].astype(f32) + sent_ref[...].astype(f32)).astype(bf16)

    return call(
        kernel, (1,), [full((rows, width))] * 2, full((rows, width)), shaped(rows, width), [],
        cost(rows * width, 6 * rows * width), low, sent,
    )


def flip(value, bit, axis="tensor"):
    count = lax.axis_size(axis)
    return lax.ppermute(value, axis, [(i, i ^ (1 << bit)) for i in range(count)])


def axis_bits(axis):
    return lax.axis_size(axis).bit_length() - 1


def reduce_rest(low, sent):
    for bit in range(1, axis_bits("tensor")):
        low, high = add_halves(low, sent)
        sent = flip(high, bit)
    return low, sent


def gather_share(share):
    parts = [share]
    for bit in reversed(range(axis_bits("tensor"))):
        parts = parts + [flip(part, bit) for part in parts]
    return parts


def half_rest(low, sent):
    for bit in range(1, axis_bits("tensor")):
        low = add_rows(low, sent)
        sent = flip(low, bit)
    return low, sent


def gather_half(half):
    return [half, flip(half, 0)]


def to_second(value):
    return lax.ppermute(value, "section", [(0, 1)])


def to_first(value):
    return lax.ppermute(value, "section", [(1, 0)])


def sum_over(value, axis):
    for bit in range(axis_bits(axis)):
        value = value + flip(value, bit, axis)
    return value


def table_rows_of(value, table, tables, half):
    return jnp.concatenate([value[(core * tables + table) * half : (core * tables + table + 1) * half] for core in range(2)], axis=0)


def in_frame(values, half):
    return jnp.concatenate([value[core * half : (core + 1) * half] for core in range(2) for value in values], axis=0)


def decoder_attend(q, keys, values, masks, w_out, outs):
    heads_out, wide_out, log_out, low, high = outs
    tables = len(keys)
    half = q.shape[0] // (2 * tables)
    wides = []
    for table in range(tables):
        wide, logs = attention_rows(table_rows_of(q, table, tables, half), keys[table], values[table], masks[table])
        wides.append(wide)
        log_out[table * 8 : table * 8 + 8] = logs[:8]
    wide = in_frame(wides, half)
    heads = wide.astype(bf16)
    wide_out[...] = wide
    heads_out[...] = heads
    partial = mm_t(heads, w_out).astype(bf16)
    low[...] = partial[: tables * half]
    high[...] = partial[tables * half :]


def attend_shapes(rows, columns, width, tables):
    shapes = [(rows, columns, bf16), (rows, columns, f32), (8 * tables, rows // tables, f32), (rows // 2, width, bf16), (rows // 2, width, bf16)]
    return [full(shape[:2]) for shape in shapes], [shaped(*shape) for shape in shapes]


def decoder_self(parts, w_q, w_k, w_v, bias, masks, w_out):
    tables = masks.shape[0]
    rows, width = 2 * parts[0].shape[0], parts[0].shape[1]
    half = rows // (2 * tables)
    columns = w_q.shape[1]

    def kernel(own, other, w_q, w_k, w_v, bias, masks, w_out, x_out, q_out, k_out, v_out, *outs):
        x = jnp.concatenate([own[...], other[...]], axis=0)
        x_out[...] = x
        q = (mm(x, w_q[...]) + bias[0:1]).astype(bf16)
        k = mm(x, w_k[...]).astype(bf16)
        v = (mm(x, w_v[...]) + bias[1:2]).astype(bf16)
        q_out[...], k_out[...], v_out[...] = q, k, v
        keys, values = ([table_rows_of(value, table, tables, half) for table in range(tables)] for value in (k, v))
        decoder_attend(q, keys, values, [masks[table] for table in range(tables)], w_out[...], outs)

    specs, shapes = attend_shapes(rows, columns, width, tables)
    return call(
        kernel, (1,),
        [full(value.shape) for value in (*parts, w_q, w_k, w_v, bias, masks, w_out)],
        [full((rows, width))] + [full((rows, columns))] * 3 + specs,
        [shaped(rows, width)] + [shaped(rows, columns)] * 3 + shapes, [],
        cost(8 * rows * width * columns, 8 * width * columns),
        *parts, w_q, w_k, w_v, bias, masks, w_out,
    )


def decoder_cross(parts, w_q, bias, keys, values, masks, w_out):
    tables = len(keys)
    rows, width = 2 * parts[0].shape[0], parts[0].shape[1]
    columns = w_q.shape[1]

    def kernel(own, other, w_q, bias, masks, w_out, *refs):
        keys, values, (x_out, q_out), outs = refs[:tables], refs[tables : 2 * tables], refs[2 * tables : 2 * tables + 2], refs[2 * tables + 2 :]
        x = jnp.concatenate([own[...], other[...]], axis=0)
        x_out[...] = x
        q = (mm(x, w_q[...]) + bias[...]).astype(bf16)
        q_out[...] = q
        decoder_attend(q, keys, values, [masks[table : table + 1] for table in range(tables)], w_out[...], outs)

    specs, shapes = attend_shapes(rows, columns, width, tables)
    return call(
        kernel, (1,),
        [full(value.shape) for value in (*parts, w_q, bias, masks, w_out, *keys, *values)],
        [full((rows, width)), full((rows, columns))] + specs,
        [shaped(rows, width), shaped(rows, columns)] + shapes, [],
        cost(4 * rows * width * columns + 4 * rows * keys[0].shape[0] * columns, 8 * width * columns),
        *parts, w_q, bias, masks, w_out, *keys, *values,
    )


def decoder_attend_back(grads, wide, logs, q, keys, values, masks):
    tables = len(keys)
    half = q.shape[0] // (2 * tables)
    dqs, dks, dvs = [], [], []
    for table in range(tables):
        dk_parts, dv_parts = [], []

        def add(at, dk, dv):
            dk_parts.append(dk.astype(bf16))
            dv_parts.append(dv.astype(bf16))

        g, w, q_rows = (table_rows_of(value, table, tables, half) for value in (grads, wide, q))
        dqs.append(attention_back_rows(g, w, logs[table * 8 : table * 8 + 8], q_rows, keys[table], values[table], masks[table], add))
        dks.append(jnp.concatenate(dk_parts, axis=1))
        dvs.append(jnp.concatenate(dv_parts, axis=1))
    return in_frame(dqs, half), dks, dvs


def rows_sum(value):
    return jnp.sum(value.astype(f32), axis=0, keepdims=True)


def decoder_cross_back(parts, w_out, wide, logs, q, keys, values, masks, w_q):
    tables = len(keys)
    rows, width = 2 * parts[0].shape[0], parts[0].shape[1]
    columns = w_q.shape[1]
    slots = keys[0].shape[0]

    def kernel(own, other, w_out, wide, logs, q, masks, w_q, *refs):
        keys, values, outs = refs[:tables], refs[tables : 2 * tables], refs[2 * tables :]
        x = jnp.concatenate([own[...], other[...]], axis=0)
        outs[0][...] = x
        grads = mm(x, w_out[...]).astype(bf16)
        columns_of = [masks[:, table : table + 1] for table in range(tables)]
        dq, dks, dvs = decoder_attend_back(grads, wide[...], logs[...], q[...], keys, values, columns_of)
        outs[1][...] = dq
        outs[2][...] = rows_sum(dq)
        partial = mm_t(dq, w_q[...]).astype(bf16)
        outs[3][...] = partial[: rows // 2]
        outs[4][...] = partial[rows // 2 :]
        total = 0.0
        for table in range(tables):
            outs[6 + table][...] = dks[table]
            outs[6 + tables + table][...] = dvs[table]
            total = total + rows_sum(dvs[table])
        outs[5][...] = total

    shapes = [(rows, width, bf16), (rows, columns, bf16), (1, columns, f32), (rows // 2, width, bf16), (rows // 2, width, bf16), (1, columns, f32)]
    shapes += [(slots, columns, bf16)] * (2 * tables)
    return call(
        kernel, (1,),
        [full(value.shape) for value in (*parts, w_out, wide, logs, q, masks, w_q, *keys, *values)],
        [full(shape[:2]) for shape in shapes], [shaped(*shape) for shape in shapes], [],
        cost(4 * rows * width * columns + 10 * rows * slots * columns, 8 * width * columns),
        *parts, w_out, wide, logs, q, masks, w_q, *keys, *values,
    )


def decoder_self_back(parts, w_out, wide, logs, q, k, v, masks, w_q, w_k, w_v):
    tables = masks.shape[0]
    rows, width = 2 * parts[0].shape[0], parts[0].shape[1]
    half = rows // (2 * tables)
    columns = w_q.shape[1]

    def kernel(own, other, w_out, wide, logs, q, k, v, masks, w_q, w_k, w_v, x_out, q_out, k_out, v_out, q_sum, v_sum, low, high):
        x = jnp.concatenate([own[...], other[...]], axis=0)
        x_out[...] = x
        grads = mm(x, w_out[...]).astype(bf16)
        keys, values = ([table_rows_of(value[...], table, tables, half) for table in range(tables)] for value in (k, v))
        dq, dks, dvs = decoder_attend_back(grads, wide[...], logs[...], q[...], keys, values, [masks[table] for table in range(tables)])
        dk, dv = in_frame(dks, half), in_frame(dvs, half)
        q_out[...], k_out[...], v_out[...] = dq, dk, dv
        q_sum[...], v_sum[...] = rows_sum(dq), rows_sum(dv)
        partial = (mm_t(dq, w_q[...]) + mm_t(dk, w_k[...]) + mm_t(dv, w_v[...])).astype(bf16)
        low[...] = partial[: rows // 2]
        high[...] = partial[rows // 2 :]

    shapes = [(rows, width, bf16)] + [(rows, columns, bf16)] * 3 + [(1, columns, f32)] * 2 + [(rows // 2, width, bf16)] * 2
    return call(
        kernel, (1,),
        [full(value.shape) for value in (*parts, w_out, wide, logs, q, k, v, masks, w_q, w_k, w_v)],
        [full(shape[:2]) for shape in shapes], [shaped(*shape) for shape in shapes], [],
        cost(12 * rows * width * columns, 8 * width * columns),
        *parts, w_out, wide, logs, q, k, v, masks, w_q, w_k, w_v,
    )


def per_device(
    table_input,
    target_input,
    cotangent,
    table_lengths,
    target_lengths,
    query_key,
    value_out,
    hidden_in,
    hidden_out,
    hidden_bias,
    vectors,
    cross_bias,
):
    sections = lax.axis_size("section")
    count = lax.axis_size("tensor")
    bits = axis_bits("tensor")
    rank = lax.axis_index("tensor")
    section = lax.axis_index("section")
    is_first = section == 0
    section_ref = section.reshape(1).astype(jnp.int32)
    in_line = lax.axis_size("dp") == CHUNKS
    order_ref = jnp.where(in_line, lax.axis_index("dp"), 0).astype(jnp.int32) ^ jnp.array(MASKS[2:] + MASKS[:2], jnp.int32)
    place_ref = jnp.where(in_line, lax.axis_index("dp"), 0).reshape(1).astype(jnp.int32)
    tables, slots, width = table_input.shape
    targets = target_input.shape[1]
    columns = query_key.shape[3]
    rows = vectors[0]
    row = [rows[index : index + 1] for index in range(rows.shape[0])]
    head_rows = lax.dynamic_slice_in_dim(rows[0:3], rank * columns, columns, 1)
    no_bias = jnp.zeros((1, columns), f32)
    w_query, w_key, w_third_q = query_key[0, 0], query_key[0, 1], query_key[0, 2]
    w_value, w_out, w_third_v = value_out[0, 0], value_out[0, 1], value_out[0, 2]
    w_in, w_hidden_out = hidden_in[0], hidden_out[0]
    w_cross_key, w_cross_value, b_cross_value = to_second(w_third_q), to_second(w_third_v), to_second(head_rows[2:3])

    masks = [int(format(p, f"0{bits}b")[::-1], 2) for p in range(count)]
    owners = rank.astype(jnp.int32) ^ jnp.array(masks, jnp.int32)
    short = slots // (sections * count)
    row_index = (
        jnp.arange(sections)[None, :, None] * (count * short)
        + owners[:, None, None] * short
        + jnp.arange(short)[None, None, :]
    ).reshape(-1)
    table_valid = row_index[None, :] < table_lengths[:, None]
    table_mask = jnp.where(table_valid, 0.0, -1e30).astype(f32)

    cores = 2
    small = targets // (sections * count)
    core_order = (rank % cores) ^ jnp.arange(cores)
    half = targets // cores

    def target_frame(value):
        split = value.reshape(tables, sections, count // cores, cores, small, width)
        split = jnp.take(split, core_order, axis=3)
        return jnp.transpose(split, (3, 0, 2, 1, 4, 5)).reshape(cores, tables * half, width)

    target_index = (
        jnp.arange(sections)[None, None, :, None] * (count * small)
        + jnp.arange(count // cores)[None, :, None, None] * (cores * small)
        + core_order[:, None, None, None] * small
        + jnp.arange(small)[None, None, None, :]
    ).reshape(-1)
    target_rows = target_frame(target_input)
    grad_rows_half = target_frame(cotangent)[0]
    target_valid = target_index[None, :] < target_lengths[:, None]
    causal = (target_index[None, :] <= target_index[:, None])[None] & target_valid[:, None, :]

    causal_mask = jnp.where(causal, 0.0, -1e30).astype(f32)
    causal_back = jnp.swapaxes(causal_mask, 1, 2)

    encoder_kept, encoder_out = {}, {}
    cross, dec, grad_memory = {}, {}, {}
    order.last = None

    def encode(table):
        first_in, queries, keys, values, normed, raw = encoder_qkv(
            table_input, table, owners, row[9], row[10], w_query, w_key, w_value, head_rows[0:2], sections
        )
        yield "qkv"
        heads, wide, logs, low, high = encoder_attention(queries, keys, values, table_mask[table][None], w_out, count)
        sent = flip(high, 0)
        yield "attention"
        parts = reduce_rest(low, sent)
        yield "reduce"
        summed_one, middle, sent = norm_forward(normed, parts, row[3], row[5], row[6])
        parts = gather_share(sent)
        yield "norm"
        yield "gather"
        second_in, hidden, slope, low, high = ffn_forward(parts, w_in, hidden_bias, w_hidden_out)
        sent = flip(high, 0)
        yield "ffn"
        parts = reduce_rest(low, sent)
        yield "reduce two"
        summed_two, _, memory = norm_forward(middle, parts, row[4], row[7], row[8])
        encoder_kept[table] = (raw, first_in, queries, keys, values, heads, wide, logs, summed_one, second_in, hidden, slope, summed_two)
        memory = to_second(memory)
        yield "memory"
        parts = gather_share(memory)
        yield "moved"
        yield "gather two"
        cross[table] = project_parts(parts, [w_cross_key, w_cross_value], [no_bias, b_cross_value])
        yield "cross"

    def decode():
        dec["first"], q, k, v, heads, wide, logs, low, high = decoder_self(
            [target_rows[0], target_rows[1]], w_query, w_key, w_value, head_rows[0:2], causal_mask, w_out
        )
        dec["self"] = (q, k, v, heads, wide, logs)
        sent = flip(high, 0)
        yield "self"
        parts = half_rest(low, sent)
        yield "reduce"
        dec["one"], middle, sent = norm_forward(target_rows[0].astype(f32), parts, row[3], row[5], row[6])
        sent = gather_half(sent)
        yield "norm"
        keys, values = [cross[table][1] for table in range(tables)], [cross[table][2] for table in range(tables)]
        cross_in, q, heads, wide, logs, low, high = decoder_cross(
            sent, w_third_q, head_rows[2:3], keys, values, table_mask, w_third_v
        )
        parts = half_rest(low, flip(high, 0))
        three, later, sent = norm_forward(middle, parts, cross_bias[None], row[9], row[10])
        third_in, hidden, slope, low, high = ffn_forward(gather_half(sent), w_in, hidden_bias, w_hidden_out)
        parts = half_rest(low, flip(high, 0))
        two, _, dec["out"] = norm_forward(later, parts, row[4], row[7], row[8])
        grad_two, sent, dec["sums_two"] = norm_backward(two, row[7], [grad_rows_half])
        grad_two_rows, before_grad, low, high, dec["bias"] = ffn_backward(gather_half(sent), slope, w_in, w_hidden_out)
        parts = half_rest(low, flip(high, 0))
        grad_three, sent, dec["sums_three"] = norm_backward(three, row[9], [grad_two, *parts])
        grad_three_rows, dq, dec["third_sum"], low, high, third_bias, *rest = decoder_cross_back(
            gather_half(sent), w_third_v, wide, logs, q, keys, values, jnp.swapaxes(table_mask, 0, 1), w_third_q
        )
        dec["cross_rows"] = low, high
        dks, dvs = rest[:tables], rest[tables:]
        for table in range(tables):
            low, high = back_sum([dks[table], dvs[table]], [w_cross_key, w_cross_value], count)
            dec["memory", table] = low, flip(high, 0)
        dec["grad_three"] = grad_three
        dec["pairs"] = {"in": [(third_in, before_grad)], "out": [(grad_two_rows, hidden)]}
        yield "back"
        memory_rows = [cross[table][0] for table in range(tables)]
        arrived = weight_sum(memory_rows, dks), weight_sum(memory_rows, dvs)
        own = weight_sum([cross_in], [dq]), weight_sum([grad_three_rows], [heads])
        yield "thirds"
        arrived = [to_first(value) for value in gate(*arrived)]
        dec["third_bias"] = to_first(third_bias)
        yield "third send"
        first, *rest = pick_third(section_ref, place_ref, arrived, own)
        if in_line:
            sent = send_chunks(rest)
        yield "third pick"
        if in_line:
            total = sum_chunks(first, sent)
            sent = send_chunks([total] * (CHUNKS - 1))
            dec["thirds"] = [total, *sent]
        else:
            totals = lax.psum([first, *rest], "dp")
            dec["thirds"] = totals[:1] + totals[:0:-1]
        yield "third sum"

    def memory_back(table):
        keep, sent = reduce_rest(*dec["memory", table])
        yield "reduce"
        grad_memory[table] = to_first(add_rows(keep, sent))
        yield "moved"

    def decode_rest():
        low, high = gate(*dec["cross_rows"])
        sent = flip(high, 0)
        yield "start"
        parts = half_rest(low, sent)
        yield "reduce"
        grad_one, sent, dec["sums_one"] = norm_backward(dec["one"], row[5], [dec["grad_three"], *parts])
        sent = gather_half(sent)
        yield "norm"
        q, k, v, heads, wide, logs = dec["self"]
        grad_one_rows, grad_q, grad_k, grad_v, dec["sum_q"], dec["sum_v"], low, high = decoder_self_back(
            sent, w_out, wide, logs, q, k, v, causal_back, w_query, w_key, w_value
        )
        first = dec["first"]
        dec["pairs"].update({"qk": [(first, grad_q), (first, grad_k)], "vo": [(first, grad_v), (grad_one_rows, heads)]})
        sent = flip(high, 0)
        yield "self"
        keep, sent = half_rest(low, sent)
        yield "reduce two"
        dec["target_grad"] = (grad_one + keep.astype(f32) + sent.astype(f32)).astype(bf16)

    def encode_back(table):
        (raw, first_in, queries, keys, values, heads, wide, logs, summed_one, second_in, hidden, slope, summed_two) = encoder_kept[table]
        grad_two, sent, sums_two = norm_backward(summed_two, row[7], [grad_memory[table]])
        parts = gather_share(sent)
        yield "norm two"
        yield "gather two"
        grad_two_rows, grad_before, low, high, bias = ffn_backward(parts, slope, w_in, w_hidden_out)
        pairs = {"in": [(second_in, grad_before)], "out": [(grad_two_rows, hidden)]}
        encoder_out[table] = pairs
        sent = flip(high, 0)
        yield "ffn"
        parts = reduce_rest(low, sent)
        yield "reduce two"
        grad_one, sent, sums_one = norm_backward(summed_one, row[5], [grad_two, *parts])
        parts = gather_share(sent)
        yield "norm one"
        yield "gather one"
        grad_one_rows, grad_q, grad_k, grad_v, sum_q, sum_v = encoder_attention_back(
            parts, wide, logs, queries, keys, values, table_mask[table][:, None], w_out
        )
        pairs.update({"qk": [(first_in, grad_q), (first_in, grad_k)], "vo": [(first_in, grad_v), (grad_one_rows, heads)]})
        yield "attention"
        low, high = back_sum([grad_q, grad_k, grad_v], [w_query, w_key, w_value], count)
        sent = flip(high, 0)
        yield "back"
        parts = reduce_rest(low, sent)
        yield "reduce one"
        _, pairs["table_grad"], sums_zero = norm_backward(raw, row[9], [grad_one, *parts])
        sums = [sums_one[2], sums_two[2], sums_one[0], sums_one[1], sums_two[0], sums_two[1], sums_zero[0], sums_zero[1]]
        pairs["sums"] = (jnp.stack(sums), sum_q[0], sum_v[0], bias)
        yield "norm zero"

    totals = {}

    def weights(name):
        totals[name] = []
        low, high = weight_grad(section_ref, order_ref, [encoder_out[table][name] for table in range(tables)], dec["pairs"][name])
        return sum_places(low, high, totals[name])

    def to(part, *labels):
        for label in labels:
            for said in part:
                if said == label:
                    break

    def each(parts, *labels):
        for label in labels:
            for part in parts:
                to(part, label)

    ahead, *behind = forward = [encode(table) for table in range(tables)]
    decoder = decode()
    to(ahead, "qkv", "attention")
    w_cross_key, w_cross_value, b_cross_value = gate(w_cross_key, w_cross_value, b_cross_value)
    each(behind, "qkv")
    to(ahead, "reduce")
    each(behind, "attention")
    to(ahead, "norm")
    each(behind, "reduce")
    to(decoder, "self", "reduce")
    to(ahead, "ffn")
    each(behind, "norm")
    to(decoder, "norm")
    to(ahead, "reduce two")
    each(behind, "ffn")
    to(ahead, "memory")
    each(behind, "reduce two", "memory")
    each(forward, "cross")

    to(decoder, "back")
    returned = [memory_back(table) for table in range(tables)]
    each(returned, "reduce")
    to(decoder, "thirds")
    each(returned, "moved")
    rest = decode_rest()

    ahead, *behind = backward = [encode_back(table) for table in range(tables)]
    to(ahead, "norm two")
    each(behind, "norm two")
    to(rest, "start")
    to(decoder, "third send")
    to(ahead, "ffn")
    to(rest, "reduce")
    to(ahead, "reduce two")
    to(decoder, "third pick")
    each(behind, "ffn")
    to(ahead, "norm one")
    each(behind, "reduce two")
    out_sum = weights("out")
    to(out_sum, "made")
    to(decoder, "third sum")
    in_sum = weights("in")
    to(in_sum, "made")
    to(rest, "norm")
    to(ahead, "attention")
    to(out_sum, "one")
    each(behind, "norm one")
    to(rest, "self")
    to(ahead, "back")
    to(in_sum, "one")
    to(rest, "reduce two")
    to(ahead, "reduce one")
    to(out_sum, "two")
    each(behind, "attention")
    to(in_sum, "two")
    qk_sum = weights("qk")
    to(qk_sum, "made")
    vo_sum = weights("vo")
    to(vo_sum, "made")
    to(out_sum, "three")
    each(behind, "back")
    to(ahead, "norm zero")
    to(in_sum, "three")
    to(qk_sum, "one")
    each(behind, "reduce one")
    to(vo_sum, "one")
    to(qk_sum, "two")
    each(behind, "norm zero")
    to(vo_sum, "two")
    to(qk_sum, "three")
    to(vo_sum, "three")
    for part in (rest, decoder, out_sum, in_sum, qk_sum, vo_sum, *backward, *forward):
        to(part, "end")

    table_grads = [encoder_out[table]["table_grad"] for table in range(tables)]
    enc_rows, enc_sum_q, enc_sum_v, enc_bias = (sum(values) for values in zip(*[encoder_out[table]["sums"] for table in range(tables)]))
    decoded, target_grad = dec["out"], dec["target_grad"]
    sums_one, sums_two, sums_three = dec["sums_one"], dec["sums_two"], dec["sums_three"]
    dec_rows = jnp.stack(
        [sums_one[2], sums_two[2], sums_one[0], sums_one[1], sums_two[0], sums_two[1], sums_three[0], sums_three[1], sums_three[2]]
    ) * (cores / count)
    dec_head_rows = [dec["sum_q"][0], dec["sum_v"][0], dec["third_sum"][0]]
    dec_bias = dec["bias"]
    third_bias_grad = dec["third_bias"][0]

    total_out, total_in = unite_one(place_ref, totals["out"]), unite_one(place_ref, totals["in"])
    query_key_grad, value_out_grad = unite(place_ref, totals["qk"], totals["vo"], dec["thirds"])

    head_sums = jnp.where(is_first, jnp.stack([enc_sum_q, enc_sum_v, third_bias_grad]), jnp.stack(dec_head_rows))
    placed = lax.dynamic_update_slice(jnp.zeros((3, width), f32), head_sums, (0, rank * columns))
    other_rows = jnp.where(is_first, jnp.pad(enc_rows, ((0, 1), (0, 0))), dec_rows)
    bias_row = jnp.pad(jnp.where(is_first, enc_bias, dec_bias), ((0, 0), (0, width - enc_bias.shape[1])))
    bundle = sum_over(jnp.concatenate([placed, other_rows, bias_row]), "dp")
    bias_sum = bundle[12:13, : enc_bias.shape[1]]
    bundle = sum_over(bundle[:12], "tensor")
    vector_total = bundle[:11]
    cross_total = bundle[11] + lax.ppermute(bundle[11], "section", [(0, 1), (1, 0)])

    table_grads = jnp.stack(table_grads).reshape(tables, sections, short, width)
    moved_up = lax.ppermute(table_grads[:, 1], "section", [(0, 1)])
    table_out = jnp.where(is_first, table_grads[:, 0], moved_up)
    own = lax.dynamic_slice_in_dim(
        jnp.stack([decoded, target_grad]).reshape(2, tables, count // cores, sections, small, width),
        rank // cores,
        1,
        2,
    )[:, :, 0]
    moved_down = lax.ppermute(own[:, :, 0], "section", [(1, 0)])
    small_out = jnp.where(is_first, moved_down, own[:, :, 1])
    return (
        small_out[0],
        table_out,
        small_out[1],
        query_key_grad[None],
        value_out_grad[None],
        total_in[None],
        total_out[None],
        bias_sum,
        vector_total[None],
        cross_total,
    )


def solution(mesh):
    in_specs = (
        P("dp", None, None),
        P("dp", None, None),
        P("dp", None, None),
        P("dp"),
        P("dp"),
        P("section", None, None, "tensor"),
        P("section", None, None, "tensor"),
        P("section", None, "tensor"),
        P("section", None, "tensor"),
        P("section", "tensor"),
        P("section", None, None),
        P(),
    )
    out_specs = (
        P("dp", ("section", "tensor"), None),
        P("dp", ("section", "tensor"), None),
        P("dp", ("section", "tensor"), None),
        P("section", None, None, "tensor"),
        P("section", None, None, "tensor"),
        P("section", None, "tensor"),
        P("section", None, "tensor"),
        P("section", "tensor"),
        P("section", None, None),
        P(),
    )
    return jax.shard_map(
        per_device, mesh=mesh, in_specs=in_specs, out_specs=out_specs, check_vma=False
    )
```

```python
import jax
import jax.numpy as jnp
from jax import lax
from jax.experimental import pallas as pl
from jax.experimental.pallas import tpu as pltpu
from jax.sharding import PartitionSpec as P

HEAD = 64
SCALING = HEAD ** (-0.5)
EPSILON = 1e-05

bf16 = jnp.bfloat16
f32 = jnp.float32


def mm(a, b):
    return lax.dot_general(a, b, (((1,), (0,)), ((), ())), preferred_element_type=f32)


def mm_t(a, b):
    return lax.dot_general(a, b, (((1,), (1,)), ((), ())), preferred_element_type=f32)


def t_mm(a, b):
    return lax.dot_general(a, b, (((0,), (0,)), ((), ())), preferred_element_type=f32)


def norm_stats(summed):
    centered = summed - jnp.mean(summed, axis=-1, keepdims=True)
    spread = jnp.mean(centered * centered, axis=-1, keepdims=True)
    scale = lax.rsqrt(spread + EPSILON)
    return centered * scale, scale


def gelu_pair(before):
    cumulative = 0.5 * (1.0 + lax.erf(before * (0.5 ** 0.5)))
    density = jnp.exp(-0.5 * before * before) * 0.3989422804014327
    return before * cumulative, cumulative + before * density


def shaped(rows, width, dtype=bf16):
    return jax.ShapeDtypeStruct((rows, width), dtype)


def full(shape):
    return pl.BlockSpec(shape, lambda *_: (0,) * len(shape))


def turned(steps):
    return lambda i, *_: ((i + steps // 2) % steps, 0)


def low_high(rows, width, steps):
    return [
        pl.BlockSpec((rows, width), lambda i, *_: (jnp.maximum(i - steps // 2, 0), 0)),
        pl.BlockSpec((rows, width), lambda i, *_: (jnp.minimum(i, steps // 2 - 1), 0)),
    ]


def put_low_high(value, low, high):
    first = pl.program_id(0) < pl.num_programs(0) // 2

    @pl.when(first)
    def _():
        high[...] = value

    @pl.when(jnp.logical_not(first))
    def _():
        low[...] = value


def pick_block(parts, held):
    steps = len(parts)
    at = (pl.program_id(0) + steps // 2) % steps
    for index, part in enumerate(parts):
        @pl.when(at == index)
        def _(part=part):
            held[...] = part[...]
    return held[...]


def cost(flops, moved, exps=0):
    return pl.CostEstimate(flops=int(flops), bytes_accessed=int(moved), transcendentals=int(exps))


ORDER = (
    ("g", "send"),
    ("e0", "qkv"),
    ("e0", "attention"),
    ("g", "gate"),
    ("e1", "qkv"),
    ("e0", "reduce"),
    ("e1", "attention"),
    ("e0", "norm"),
    ("e1", "reduce"),
    ("d", "self"),
    ("d", "reduce"),
    ("e0", "ffn"),
    ("e1", "norm"),
    ("d", "norm"),
    ("e0", "reduce two"),
    ("e1", "ffn"),
    ("e0", "memory"),
    ("e1", "reduce two"),
    ("e1", "memory"),
    ("e0", "cross"),
    ("e1", "cross"),
    ("d", "back"),
    ("m0", "reduce"),
    ("m1", "reduce"),
    ("d", "thirds"),
    ("m0", "moved"),
    ("m1", "moved"),
    ("b0", "norm two"),
    ("b1", "norm two"),
    ("r", "start"),
    ("d", "third send"),
    ("b0", "ffn"),
    ("r", "reduce"),
    ("b0", "reduce two"),
    ("d", "third pick"),
    ("b1", "ffn"),
    ("b0", "norm one"),
    ("b1", "reduce two"),
    ("out", "made"),
    ("d", "third sum"),
    ("in", "made"),
    ("r", "norm"),
    ("b0", "attention"),
    ("b1", "norm one"),
    ("r", "self"),
    ("b0", "back"),
    ("r", "reduce two"),
    ("b0", "reduce one"),
    ("out", "one"),
    ("b1", "attention"),
    ("out", "two"),
    ("qk", "made"),
    ("vo", "made"),
    ("in", "one"),
    ("b1", "back"),
    ("d", "third end"),
    ("b0", "norm zero"),
    ("out", "three"),
    ("b1", "reduce one"),
    ("in", "two"),
    ("b1", "norm zero"),
    ("qk", "one"),
    ("vo", "one"),
    ("in", "three"),
    ("out", "four"),
    ("qk", "two"),
    ("vo", "two"),
    ("in", "four"),
    ("qk", "three"),
    ("vo", "three"),
)


class Order:
    def __init__(self):
        self.last = None


order = Order()


def call(kernel, grid, in_specs, out_specs, out_shape, scratch, estimate, *args, prefetch=()):
    count = len(prefetch) + len(args)
    after = [] if order.last is None else [order.last]

    def ordered(*refs):
        kernel(*refs[:count], *refs[count + len(after) :])

    grid_spec = pltpu.PrefetchScalarGridSpec(
        num_scalar_prefetch=len(prefetch),
        grid=grid,
        in_specs=list(in_specs) + [pl.BlockSpec(memory_space=pl.ANY)] * len(after),
        out_specs=out_specs,
        scratch_shapes=scratch,
    )
    results = pl.pallas_call(
        ordered,
        grid_spec=grid_spec,
        out_shape=out_shape,
        compiler_params=pltpu.CompilerParams(vmem_limit_bytes=48 * 1024 * 1024),
        cost_estimate=estimate,
        name=kernel.__qualname__.split(".")[0],
    )(*prefetch, *args, *after)
    order.last = min(results, key=lambda result: result.size) if isinstance(results, (list, tuple)) else results
    return results


def gate(*values, behind=()):
    count = len(values)
    after = ([] if order.last is None else [order.last]) + list(behind)
    results = pl.pallas_call(
        lambda *refs: None,
        in_specs=[pl.BlockSpec(memory_space=pl.ANY)] * (count + len(after)),
        out_specs=[pl.BlockSpec(memory_space=pl.ANY)] * count,
        out_shape=[jax.ShapeDtypeStruct(value.shape, value.dtype) for value in values],
        input_output_aliases={index: index for index in range(count)},
        cost_estimate=cost(0, 0),
        name="gate",
    )(*values, *after)
    order.last = results[0]
    return results if count > 1 else results[0]


def norm_kernel(residual, keep, sent, bias, gain, shift, summed_out, wide_out, out):
    summed = residual[...] + (keep[...].astype(f32) + sent[...].astype(f32)) + bias[...]
    normed = norm_stats(summed)[0] * gain[...] + shift[...]
    summed_out[...] = summed
    wide_out[...] = normed
    out[...] = normed.astype(bf16)


def norm_forward(residual, parts, bias, gain, shift):
    rows, width = residual.shape
    block, row = full((rows, width)), full((1, width))
    return call(
        norm_kernel, (1,), [block] * 3 + [row] * 3, [block] * 3,
        [shaped(rows, width, f32)] * 2 + [shaped(rows, width)], [],
        cost(12 * rows * width, 18 * rows * width),
        residual, *parts, bias, gain, shift,
    )


def norm_back_kernel(count, *refs):
    grads, (summed, gain, wide_out, out, sums) = refs[:count], refs[count:]
    gradient = grads[0][...].astype(f32)
    for grad in grads[1:]:
        gradient = gradient + grad[...].astype(f32)
    unit, scale = norm_stats(summed[...].astype(f32))
    scaled = gradient * gain[...]
    inner = scaled - jnp.mean(scaled, axis=-1, keepdims=True)
    inner = (inner - unit * jnp.mean(scaled * unit, axis=-1, keepdims=True)) * scale
    wide_out[...] = inner
    out[...] = inner.astype(bf16)
    sums[...] = jnp.concatenate(
        [
            jnp.sum(gradient * unit, axis=0, keepdims=True),
            jnp.sum(gradient, axis=0, keepdims=True),
            jnp.sum(inner, axis=0, keepdims=True),
            jnp.zeros((5, inner.shape[1]), f32),
        ]
    )


def norm_backward(summed, gain, grads):
    rows, width = summed.shape
    block, row = full((rows, width)), full((1, width))

    def kernel(*refs):
        norm_back_kernel(len(grads), *refs)

    return call(
        kernel, (1,), [block] * (len(grads) + 1) + [row], [block] * 2 + [full((8, width))],
        [shaped(rows, width, f32), shaped(rows, width), shaped(8, width, f32)], [],
        cost(20 * rows * width, 18 * rows * width),
        *grads, summed, gain,
    )


def qkv_kernel(sections, owners, *refs):
    parts = refs[:sections]
    gain, shift, w_q, w_k, w_v, bias, x_out, q_out, k_out, v_out, own_norm, own_raw = refs[sections:]
    raw = jnp.concatenate([part[...] for part in parts], axis=0)
    normed = norm_stats(raw.astype(f32))[0] * gain[...] + shift[...]
    x = normed.astype(bf16)
    x_out[...] = x
    q_out[...] = (mm(x, w_q[...]) + bias[0:1]).astype(bf16)
    k_out[...] = mm(x, w_k[...]).astype(bf16)
    v_out[...] = (mm(x, w_v[...]) + bias[1:2]).astype(bf16)

    @pl.when(pl.program_id(0) == 0)
    def _():
        own_norm[...] = normed
        own_raw[...] = raw


def encoder_qkv(table_rows, table, owners, gain, shift, w_q, w_k, w_v, bias, sections):
    slots, width = table_rows.shape[1:]
    count = owners.shape[0]
    short = slots // (sections * count)
    share = sections * short
    columns = w_q.shape[1]

    def part_spec(s):
        return pl.BlockSpec((None, short, width), lambda i, order: (table, s * count + order[i], 0))

    def block(columns):
        return pl.BlockSpec((share, columns), lambda i, order: (i, 0))

    def kernel(*refs):
        qkv_kernel(sections, *refs)

    return call(
        kernel, (count,),
        [part_spec(s) for s in range(sections)] + [full((1, width))] * 2 + [full((width, columns))] * 3 + [full(bias.shape)],
        [block(width)] + [block(columns)] * 3 + [full((share, width))] * 2,
        [shaped(slots, width)] + [shaped(slots, columns)] * 3 + [shaped(share, width, f32), shaped(share, width)],
        [],
        cost(6 * slots * width * columns, 8 * slots * width),
        *([table_rows] * sections), gain, shift, w_q, w_k, w_v, bias,
        prefetch=[owners],
    )


def pair_mask(head):
    return (lax.broadcasted_iota(jnp.int32, (1, 128), 1) // HEAD) == head


def attention_rows(q_all, k_all, v_all, mask):
    rows, columns = q_all.shape
    lanes = lax.broadcasted_iota(jnp.int32, (rows, 128), 1)
    logs = jnp.zeros((rows, 128), f32)
    parts = []
    for pair in range(columns // 128):
        at = slice(pair * 128, pair * 128 + 128)
        q = q_all[:, at] * jnp.asarray(SCALING, bf16)
        k, v = k_all[:, at], v_all[:, at]
        outs = []
        for head in range(2):
            scores = mm_t(jnp.where(pair_mask(head), q, jnp.zeros_like(q)), k) + mask
            largest = jnp.max(scores, axis=-1, keepdims=True)
            exponent = jnp.exp(scores - largest)
            total = jnp.sum(exponent, axis=-1, keepdims=True)
            outs.append(mm(exponent.astype(bf16), v) / total)
            logs = jnp.where(lanes == pair * 2 + head, largest + jnp.log(total), logs)
        parts.append(jnp.where(pair_mask(0), outs[0], outs[1]))
    return jnp.concatenate(parts, axis=1), jnp.transpose(logs)


def attention_kernel(q_ref, k_ref, v_ref, mask_ref, w_out, heads_out, wide_out, log_out, low, high):
    wide, logs = attention_rows(q_ref[...], k_ref, v_ref, mask_ref[...])
    heads = wide.astype(bf16)
    wide_out[...] = wide
    heads_out[...] = heads
    log_out[...] = logs[: log_out.shape[0]]
    put_low_high(mm_t(heads, w_out[...]).astype(bf16), low, high)


def encoder_attention(queries, keys, values, mask, w_out, steps):
    slots, columns = queries.shape
    width = w_out.shape[0]
    rows = slots // steps
    block = pl.BlockSpec((rows, columns), turned(steps))
    return call(
        attention_kernel, (steps,),
        [block, full((slots, columns)), full((slots, columns)), full((1, slots)), full((width, columns))],
        [block, block, pl.BlockSpec((8, rows), lambda i: (0, (i + steps // 2) % steps))] + low_high(rows, width, steps),
        [shaped(slots, columns), shaped(slots, columns, f32), shaped(8, slots, f32)] + [shaped(slots // 2, width)] * 2,
        [],
        cost(8 * slots * slots * columns, 8 * slots * columns + 2 * slots * width, slots * slots * columns // HEAD),
        queries, keys, values, mask, w_out,
    )


def attention_back_rows(grads, wide, logs, q_all, k_all, v_all, mask, add):
    inner = jnp.transpose(grads.astype(f32) * wide)
    sub = lax.broadcasted_iota(jnp.int32, (128, 1), 0) // HEAD
    parts = []
    for pair in range(grads.shape[1] // 128):
        at = slice(pair * 128, pair * 128 + 128)
        q = q_all[:, at] * jnp.asarray(SCALING, bf16)
        k, v, g = k_all[:, at], v_all[:, at], grads[:, at]
        dk, dv, dq = 0.0, 0.0, []
        for head in range(2):
            keep = pair_mask(head)
            q_one = jnp.where(keep, q, jnp.zeros_like(q))
            g_one = jnp.where(keep, g, jnp.zeros_like(g))
            at_head = pair * 2 + head
            probability = jnp.exp((mm_t(k, q_one) + mask) - logs[at_head : at_head + 1, :])
            dv = dv + mm(probability.astype(bf16), g_one)
            delta = jnp.sum(inner[at_head * HEAD : (at_head + 1) * HEAD], axis=0, keepdims=True)
            scores_grad = (probability * (mm_t(v, g_one) - delta)).astype(bf16)
            dk = dk + mm(scores_grad, q_one)
            dq.append(t_mm(k, scores_grad))
        add(at, dk, dv)
        parts.append(jnp.transpose(jnp.where(sub == 0, dq[0], dq[1]) * SCALING))
    return jnp.concatenate(parts, axis=1).astype(bf16)


def attention_back_kernel(steps, *refs):
    parts = refs[:steps]
    (wide_ref, log_ref, q_ref, k_ref, v_ref, mask_ref, w_out, rows_out, dq_out, dk_out, dv_out, q_sum, v_sum, held, dk_sum, dv_sum) = refs[steps:]
    step = pl.program_id(0)
    grad_rows = pick_block(parts, held)
    rows_out[...] = grad_rows
    grads = mm(grad_rows, w_out[...]).astype(bf16)

    @pl.when(step == 0)
    def _():
        dk_sum[...] = jnp.zeros_like(dk_sum)
        dv_sum[...] = jnp.zeros_like(dv_sum)
        q_sum[...] = jnp.zeros_like(q_sum)

    def add(at, dk, dv):
        dk_sum[:, at] += dk
        dv_sum[:, at] += dv

    dq = attention_back_rows(grads, wide_ref[...], log_ref, q_ref[...], k_ref, v_ref, mask_ref[...], add)
    dq_out[...] = dq
    q_sum[...] += jnp.sum(dq.astype(f32), axis=0, keepdims=True)

    @pl.when(step == steps - 1)
    def _():
        dk_out[...] = dk_sum[...].astype(bf16)
        dv = dv_sum[...].astype(bf16)
        dv_out[...] = dv
        v_sum[...] = jnp.sum(dv.astype(f32), axis=0, keepdims=True)


def encoder_attention_back(grad_parts, wide, logs, queries, keys, values, mask, w_out):
    slots, columns = queries.shape
    width = w_out.shape[0]
    steps = len(grad_parts)
    rows = slots // steps
    whole, row = full((slots, columns)), full((1, columns))
    block = pl.BlockSpec((rows, columns), turned(steps))

    def kernel(*refs):
        attention_back_kernel(steps, *refs)

    return call(
        kernel, (steps,),
        [full((rows, width))] * steps
        + [block, pl.BlockSpec((8, rows), lambda i: (0, (i + steps // 2) % steps)), block, whole, whole, full((slots, 1)), full((width, columns))],
        [pl.BlockSpec((rows, width), turned(steps)), block, whole, whole, row, row],
        [shaped(slots, width)] + [shaped(slots, columns)] * 3 + [shaped(1, columns, f32)] * 2,
        [pltpu.VMEM((rows, width), bf16)] + [pltpu.VMEM((slots, columns), f32)] * 2,
        cost(20 * slots * slots * columns, 16 * slots * columns + 2 * slots * width, slots * slots * columns // HEAD),
        *grad_parts, wide, logs, queries, keys, values, mask, w_out,
    )


def ffn_kernel(steps, *refs):
    parts, (w_in, bias, w_out, x_out, hidden_out, slope_out, low, high, held) = refs[:steps], refs[steps:]
    x = pick_block(parts, held)
    x_out[...] = x
    hidden, slope = gelu_pair(mm(x, w_in[...]) + bias[...])
    hidden = hidden.astype(bf16)
    hidden_out[...] = hidden
    slope_out[...] = slope.astype(bf16)
    put_low_high(mm_t(hidden, w_out[...]).astype(bf16), low, high)


def ffn_forward(parts, w_in, bias, w_out):
    steps = len(parts)
    rows, width = parts[0].shape
    slots = rows * steps
    units = w_in.shape[1]
    block = pl.BlockSpec((rows, units), turned(steps))

    def kernel(*refs):
        ffn_kernel(steps, *refs)

    return call(
        kernel, (steps,),
        [full((rows, width))] * steps + [full((width, units)), full((1, units)), full((width, units))],
        [pl.BlockSpec((rows, width), turned(steps)), block, block] + low_high(rows, width, steps),
        [shaped(slots, width)] + [shaped(slots, units)] * 2 + [shaped(slots // 2, width)] * 2,
        [pltpu.VMEM((rows, width), bf16)],
        cost(4 * slots * width * units, 8 * slots * units + 4 * units * width, 2 * slots * units),
        *parts, w_in, bias, w_out,
    )


def ffn_back_kernel(steps, *refs):
    parts, (slope, w_in, w_out, x_out, before_out, low, high, bias_out, held) = refs[:steps], refs[steps:]
    x = pick_block(parts, held)
    x_out[...] = x
    before = (mm(x, w_out[...]) * slope[...].astype(f32)).astype(bf16)
    before_out[...] = before

    @pl.when(pl.program_id(0) == 0)
    def _():
        bias_out[...] = jnp.zeros_like(bias_out)

    bias_out[...] += jnp.sum(before.astype(f32), axis=0, keepdims=True)
    put_low_high(mm_t(before, w_in[...]).astype(bf16), low, high)


def ffn_backward(parts, slope, w_in, w_out):
    steps = len(parts)
    rows, width = parts[0].shape
    slots = rows * steps
    units = w_in.shape[1]
    block = pl.BlockSpec((rows, units), turned(steps))

    def kernel(*refs):
        ffn_back_kernel(steps, *refs)

    return call(
        kernel, (steps,),
        [full((rows, width))] * steps + [block, full((width, units)), full((width, units))],
        [pl.BlockSpec((rows, width), turned(steps)), block] + low_high(rows, width, steps) + [full((1, units))],
        [shaped(slots, width), shaped(slots, units)] + [shaped(slots // 2, width)] * 2 + [shaped(1, units, f32)],
        [pltpu.VMEM((rows, width), bf16)],
        cost(4 * slots * width * units, 6 * slots * units + 4 * units * width),
        *parts, slope, w_in, w_out,
    )


def back_sum(values, matrices, steps):
    slots, columns = values[0].shape
    width = matrices[0].shape[0]
    rows = slots // steps
    count = len(values)

    def kernel(*refs):
        total = 0.0
        for value, matrix in zip(refs[:count], refs[count : 2 * count]):
            total = total + mm_t(value[...], matrix[...])
        put_low_high(total.astype(bf16), *refs[2 * count :])

    return call(
        kernel, (steps,),
        [pl.BlockSpec((rows, columns), turned(steps))] * count + [full((width, columns))] * count,
        low_high(rows, width, steps),
        [shaped(slots // 2, width)] * 2, [],
        cost(2 * count * slots * width * columns, 2 * slots * width),
        *values, *matrices,
    )


def project_parts(parts, matrices, biases):
    steps = len(parts)
    rows, width = parts[0].shape
    slots = rows * steps
    columns = matrices[0].shape[1]
    count = len(matrices)

    def kernel(*refs):
        held = refs[-1]
        x = pick_block(refs[:steps], held)
        inner = refs[steps:-1]
        inner[2 * count][...] = x
        for index in range(count):
            inner[2 * count + 1 + index][...] = (mm(x, inner[index][...]) + inner[count + index][...]).astype(bf16)

    return call(
        kernel, (steps,),
        [full((rows, width))] * steps + [full((width, columns))] * count + [full((1, columns))] * count,
        [pl.BlockSpec((rows, width), turned(steps))] + [pl.BlockSpec((rows, columns), turned(steps))] * count,
        [shaped(slots, width)] + [shaped(slots, columns)] * count,
        [pltpu.VMEM((rows, width), bf16)],
        cost(2 * count * slots * width * columns, 4 * slots * width),
        *parts, *matrices, *biases,
    )


CHUNKS = 4


def weight_grad(section, order_ref, enc_pairs, dec_pairs):
    pairs = [(x if isinstance(x, tuple) else (x,), g) for one in (*enc_pairs, dec_pairs) for x, g in one]
    width = pairs[0][0][0].shape[1]
    chunk = width // CHUNKS
    tables, count = len(enc_pairs), len(dec_pairs)
    total_columns = sum(g.shape[1] for _, g in dec_pairs)
    starts, in_specs, args = [], [], []
    for x, g in pairs:
        starts.append(len(args))
        in_specs += [pl.BlockSpec((part.shape[0], chunk), lambda i, s, at: (0, at[i])) for part in x] + [full(g.shape)]
        args += [*x, g]

    def kernel(at, order_at, *refs):
        out = refs[-1]

        def one_product(index):
            start, blocks = starts[index], len(pairs[index][0])
            x = jnp.concatenate([ref[...] for ref in refs[start : start + blocks]], axis=0) if blocks > 1 else refs[start][...]
            return t_mm(x, refs[start + blocks][...])

        def product(index):
            return jnp.concatenate([one_product(index * count + one) for one in range(count)], axis=1)

        @pl.when(at[0] == 0)
        def _():
            total = 0.0
            for table in range(tables):
                total = total + product(table)
            out[...] = total.astype(bf16)

        @pl.when(at[0] != 0)
        def _():
            out[...] = product(tables).astype(bf16)

    rows = sum(g.shape[0] for _, g in pairs) // count
    return call(
        kernel, (CHUNKS,), in_specs,
        pl.BlockSpec((None, chunk, total_columns), lambda i, *_: (i, 0, 0)),
        jax.ShapeDtypeStruct((CHUNKS, chunk, total_columns), bf16), [],
        cost(2 * rows * width * total_columns, 2 * rows * (width + total_columns)),
        *args,
        prefetch=[section, order_ref],
    )


def sum_line(rows, parts):
    half = (CHUNKS // 2, *rows.shape[1:])
    if lax.axis_size("dp") != CHUNKS:
        rows = lax.psum(rows, "dp")
        parts.extend([rows[: CHUNKS // 2], rows[CHUNKS // 2 :]] * 2)
        return
    inward, across, outward = [(0, 1), (3, 2)], [(1, 2), (2, 1)], [(1, 0), (2, 3)]
    sent = lax.ppermute(rows, "dp", inward)
    yield "made"

    def block(shape):
        return pl.BlockSpec(shape, lambda *_: (0, 0, 0))

    def add_side(rows_ref, sent_ref, own, other):
        for index in range(CHUNKS):
            total = (rows_ref[index].astype(f32) + sent_ref[index].astype(f32)).astype(bf16)
            (own if index < CHUNKS // 2 else other)[index % (CHUNKS // 2)] = total

    own, other = call(
        add_side, (1,), [block(rows.shape)] * 2, [block(half)] * 2, [jax.ShapeDtypeStruct(half, bf16)] * 2, [],
        cost(0, 6 * rows.size), rows, sent,
    )
    sent = lax.ppermute(other, "dp", across)
    yield "one"

    def add_across(own_ref, sent_ref, out):
        for index in range(CHUNKS // 2):
            out[index] = (own_ref[index].astype(f32) + sent_ref[index].astype(f32)).astype(bf16)

    total = call(
        add_across, (1,), [block(half)] * 2, block(half), jax.ShapeDtypeStruct(half, bf16), [], cost(0, 3 * rows.size), own, sent
    )
    crossed = lax.ppermute(total, "dp", across)
    first = lax.ppermute(total, "dp", outward)
    yield "two"
    crossed, first = gate(crossed, first)
    second = lax.ppermute(crossed, "dp", outward)
    parts.extend([total, crossed, first, second])
    yield "three"


def put_chunk(line, parts, put):
    step = pl.program_id(0)
    other = (step // (CHUNKS // 2)) ^ line[0]
    for index, part in enumerate(parts):
        @pl.when(jnp.logical_and(other == index % 2, line[1] == 1 - index // 2))
        def _(part=part):
            put(part[step % (CHUNKS // 2)])


def unite_one(line, parts):
    half, chunk, columns = parts[0].shape

    def kernel(line_at, *refs):
        def put(value):
            refs[-1][...] = value.astype(f32)

        put_chunk(line_at, refs[:-1], put)

    return call(
        kernel, (CHUNKS,), [pl.BlockSpec(parts[0].shape, lambda *_: (0, 0, 0))] * 4,
        pl.BlockSpec((chunk, columns), lambda i, *_: (i, 0)),
        shaped(CHUNKS * chunk, columns, f32), [], cost(0, 24 * chunk * columns), *parts,
        prefetch=[line],
    )


def pick_third(section, place, arrived, own):
    width, columns = own[0].shape
    rows = width // CHUNKS

    def kernel(at, place_at, *refs):
        turn = (pl.program_id(0) - place_at[0]) % CHUNKS
        first = at[0] == 0
        value = jnp.concatenate([jnp.where(first, a[...], b[...]) for a, b in zip(refs[:2], refs[2:4])], axis=1)
        for index in range(CHUNKS):
            @pl.when(turn == index)
            def _(index=index):
                refs[4 + index][...] = value

    block = pl.BlockSpec((rows, columns), lambda i, *_: (i, 0))
    return call(
        kernel, (CHUNKS,), [block] * 4, [full((rows, 2 * columns))] * CHUNKS, [shaped(rows, 2 * columns)] * CHUNKS, [],
        cost(0, 8 * width * columns), *arrived, *own,
        prefetch=[section, place],
    )


def send_chunks(chunks):
    return [lax.ppermute(chunk, "dp", [(i, (i + s + 1) % CHUNKS) for i in range(CHUNKS)]) for s, chunk in enumerate(chunks)]


def sum_chunks(own, sent):
    def kernel(*refs):
        total = refs[0][...].astype(f32)
        for ref in refs[1:-1]:
            total = total + ref[...].astype(f32)
        refs[-1][...] = total.astype(bf16)

    return call(
        kernel, (1,), [full(own.shape)] * CHUNKS, full(own.shape), shaped(*own.shape), [], cost(0, 10 * own.size), own, *sent
    )


def unite(place, line, qk, vo, thirds):
    rows, columns = qk[0].shape[1], qk[0].shape[2] // 2

    def kernel(place_at, line_at, *refs):
        qk, vo, chunks, (first, second) = refs[:4], refs[4:8], refs[8 : 8 + CHUNKS], refs[8 + CHUNKS :]
        for parts, out in ((qk, first), (vo, second)):
            def put(value, out=out):
                out[0] = value[:, :columns].astype(f32)
                out[1] = value[:, columns:].astype(f32)

            put_chunk(line_at, parts, put)
        turn = (place_at[0] - pl.program_id(0)) % CHUNKS
        for index in range(CHUNKS):
            @pl.when(turn == index)
            def _(index=index):
                first[2] = chunks[index][:, :columns].astype(f32)
                second[2] = chunks[index][:, columns:].astype(f32)

    stacked = pl.BlockSpec((3, rows, columns), lambda i, *_: (0, i, 0))
    return call(
        kernel, (CHUNKS,),
        [pl.BlockSpec(qk[0].shape, lambda *_: (0, 0, 0))] * 8 + [full((rows, 2 * columns))] * CHUNKS, [stacked] * 2,
        [jax.ShapeDtypeStruct((3, CHUNKS * rows, columns), f32)] * 2, [],
        cost(0, 36 * CHUNKS * rows * columns), *qk, *vo, *thirds,
        prefetch=[place, line],
    )


def vector_rows(section, rank, encoder, third_bias, decoder, factor):
    width = decoder[0].shape[1]
    columns, units = decoder[3].shape[1], decoder[6].shape[1]
    args = [value for one in encoder for value in one] + [third_bias, *decoder]
    tables, each = len(encoder), len(encoder[0])

    def kernel(at, rank_at, *refs):
        out = refs[-1]
        out[...] = jnp.zeros_like(out)

        def put(one, two, last, heads, bias, scale):
            picked = [one[2:3], two[2:3], one[0:1], one[1:2], two[0:1], two[1:2], last[0:1], last[1:2]]
            for index, value in enumerate(picked):
                out[3 + index : 4 + index, :] = value * scale
            out[12:13, :units] = bias
            for place in range(width // columns):
                @pl.when(rank_at[0] == place)
                def _(place=place):
                    for index, value in enumerate(heads):
                        out[index : index + 1, place * columns : (place + 1) * columns] = value

        @pl.when(at[0] == 0)
        def _():
            one, two, last, q, v, bias = (sum(refs[table * each + index][...] for table in range(tables)) for index in range(each))
            put(one, two, last, (q, v, refs[tables * each][...]), bias, 1.0)

        @pl.when(at[0] != 0)
        def _():
            one, two, last, q, v, third, bias = (ref[...] for ref in refs[tables * each + 1 : -1])
            put(one, two, last, (q, v, third), bias, factor)
            out[11:12, :] = last[2:3] * factor

    return call(
        kernel, (1,), [full(value.shape) for value in args], full((16, width)), shaped(16, width, f32), [], cost(0, 200 * width),
        *args, prefetch=[section, rank],
    )


def weight_sum(xs, gs):
    count = len(xs)
    width, columns = xs[0].shape[1], gs[0].shape[1]

    def kernel(*refs):
        total = t_mm(refs[0][...], refs[count][...])
        for index in range(1, count):
            total = total + t_mm(refs[index][...], refs[count + index][...])
        refs[-1][...] = total.astype(bf16)

    rows = sum(x.shape[0] for x in xs)
    return call(
        kernel, (1,), [full(value.shape) for value in (*xs, *gs)], full((width, columns)), shaped(width, columns), [],
        cost(2 * rows * width * columns, 2 * rows * (width + columns)),
        *xs, *gs,
    )


def add_halves(low, sent):
    rows, width = low.shape[0] // 2, low.shape[1]

    def kernel(low_ref, sent_ref, low_out, high_out):
        total = (low_ref[...].astype(f32) + sent_ref[...].astype(f32)).astype(bf16)
        low_out[...] = total[:rows]
        high_out[...] = total[rows:]

    return call(
        kernel, (1,), [full((2 * rows, width))] * 2, [full((rows, width))] * 2, [shaped(rows, width)] * 2, [],
        cost(2 * rows * width, 12 * rows * width), low, sent,
    )


def add_rows(low, sent):
    rows, width = low.shape

    def kernel(low_ref, sent_ref, out):
        out[...] = (low_ref[...].astype(f32) + sent_ref[...].astype(f32)).astype(bf16)

    return call(
        kernel, (1,), [full((rows, width))] * 2, full((rows, width)), shaped(rows, width), [],
        cost(rows * width, 6 * rows * width), low, sent,
    )


def flip(value, bit, axis="tensor"):
    count = lax.axis_size(axis)
    return lax.ppermute(value, axis, [(i, i ^ (1 << bit)) for i in range(count)])


def axis_bits(axis):
    return lax.axis_size(axis).bit_length() - 1


def reduce_rest(low, sent):
    for bit in range(1, axis_bits("tensor")):
        low, high = add_halves(low, sent)
        sent = flip(high, bit)
    return low, sent


def gather_start(share):
    return [share] + [flip(share, bit) for bit in reversed(range(axis_bits("tensor")))]


def gather_rest(started):
    parts, first = [started[0]], started[1:]
    for index, bit in enumerate(reversed(range(axis_bits("tensor")))):
        parts = parts + [first[index]] + [flip(part, bit) for part in parts[1:]]
    return parts


def half_rest(low, sent):
    for bit in range(1, axis_bits("tensor")):
        low = add_rows(low, sent)
        sent = flip(low, bit)
    return low, sent


def gather_half(half):
    return [half, flip(half, 0)]


def to_second(value):
    return lax.ppermute(value, "section", [(0, 1)])


def to_first(value):
    return lax.ppermute(value, "section", [(1, 0)])


def sum_over(value, axis):
    for bit in range(axis_bits(axis)):
        value = value + flip(value, bit, axis)
    return value


def table_rows_of(value, table, tables, half):
    return jnp.concatenate([value[(core * tables + table) * half : (core * tables + table + 1) * half] for core in range(2)], axis=0)


def in_frame(values, half):
    return jnp.concatenate([value[core * half : (core + 1) * half] for core in range(2) for value in values], axis=0)


def decoder_attend(q, keys, values, masks, w_out, outs):
    heads_out, wide_out, log_out, low, high = outs
    tables = len(keys)
    half = q.shape[0] // (2 * tables)
    wides = []
    for table in range(tables):
        wide, logs = attention_rows(table_rows_of(q, table, tables, half), keys[table], values[table], masks[table])
        wides.append(wide)
        log_out[table * 8 : table * 8 + 8] = logs[:8]
    wide = in_frame(wides, half)
    heads = wide.astype(bf16)
    wide_out[...] = wide
    heads_out[...] = heads
    partial = mm_t(heads, w_out).astype(bf16)
    low[...] = partial[: tables * half]
    high[...] = partial[tables * half :]


def attend_shapes(rows, columns, width, tables):
    shapes = [(rows, columns, bf16), (rows, columns, f32), (8 * tables, rows // tables, f32), (rows // 2, width, bf16), (rows // 2, width, bf16)]
    return [full(shape[:2]) for shape in shapes], [shaped(*shape) for shape in shapes]


def decoder_self(parts, w_q, w_k, w_v, bias, masks, w_out):
    tables = masks.shape[0]
    rows, width = 2 * parts[0].shape[0], parts[0].shape[1]
    half = rows // (2 * tables)
    columns = w_q.shape[1]

    def kernel(own, other, w_q, w_k, w_v, bias, masks, w_out, x_out, q_out, k_out, v_out, *outs):
        x = jnp.concatenate([own[...], other[...]], axis=0)
        x_out[...] = x
        q = (mm(x, w_q[...]) + bias[0:1]).astype(bf16)
        k = mm(x, w_k[...]).astype(bf16)
        v = (mm(x, w_v[...]) + bias[1:2]).astype(bf16)
        q_out[...], k_out[...], v_out[...] = q, k, v
        keys, values = ([table_rows_of(value, table, tables, half) for table in range(tables)] for value in (k, v))
        decoder_attend(q, keys, values, [masks[table] for table in range(tables)], w_out[...], outs)

    specs, shapes = attend_shapes(rows, columns, width, tables)
    return call(
        kernel, (1,),
        [full(value.shape) for value in (*parts, w_q, w_k, w_v, bias, masks, w_out)],
        [full((rows, width))] + [full((rows, columns))] * 3 + specs,
        [shaped(rows, width)] + [shaped(rows, columns)] * 3 + shapes, [],
        cost(8 * rows * width * columns, 8 * width * columns),
        *parts, w_q, w_k, w_v, bias, masks, w_out,
    )


def decoder_cross(parts, w_q, bias, keys, values, masks, w_out):
    tables = len(keys)
    rows, width = 2 * parts[0].shape[0], parts[0].shape[1]
    columns = w_q.shape[1]

    def kernel(own, other, w_q, bias, masks, w_out, *refs):
        keys, values, (x_out, q_out), outs = refs[:tables], refs[tables : 2 * tables], refs[2 * tables : 2 * tables + 2], refs[2 * tables + 2 :]
        x = jnp.concatenate([own[...], other[...]], axis=0)
        x_out[...] = x
        q = (mm(x, w_q[...]) + bias[...]).astype(bf16)
        q_out[...] = q
        decoder_attend(q, keys, values, [masks[table : table + 1] for table in range(tables)], w_out[...], outs)

    specs, shapes = attend_shapes(rows, columns, width, tables)
    return call(
        kernel, (1,),
        [full(value.shape) for value in (*parts, w_q, bias, masks, w_out, *keys, *values)],
        [full((rows, width)), full((rows, columns))] + specs,
        [shaped(rows, width), shaped(rows, columns)] + shapes, [],
        cost(4 * rows * width * columns + 4 * rows * keys[0].shape[0] * columns, 8 * width * columns),
        *parts, w_q, bias, masks, w_out, *keys, *values,
    )


def decoder_attend_back(grads, wide, logs, q, keys, values, masks):
    tables = len(keys)
    half = q.shape[0] // (2 * tables)
    dqs, dks, dvs = [], [], []
    for table in range(tables):
        dk_parts, dv_parts = [], []

        def add(at, dk, dv):
            dk_parts.append(dk.astype(bf16))
            dv_parts.append(dv.astype(bf16))

        g, w, q_rows = (table_rows_of(value, table, tables, half) for value in (grads, wide, q))
        dqs.append(attention_back_rows(g, w, logs[table * 8 : table * 8 + 8], q_rows, keys[table], values[table], masks[table], add))
        dks.append(jnp.concatenate(dk_parts, axis=1))
        dvs.append(jnp.concatenate(dv_parts, axis=1))
    return in_frame(dqs, half), dks, dvs


def rows_sum(value):
    return jnp.sum(value.astype(f32), axis=0, keepdims=True)


def decoder_cross_back(parts, w_out, wide, logs, q, keys, values, masks, w_q):
    tables = len(keys)
    rows, width = 2 * parts[0].shape[0], parts[0].shape[1]
    columns = w_q.shape[1]
    slots = keys[0].shape[0]

    def kernel(own, other, w_out, wide, logs, q, masks, w_q, *refs):
        keys, values, outs = refs[:tables], refs[tables : 2 * tables], refs[2 * tables :]
        x = jnp.concatenate([own[...], other[...]], axis=0)
        outs[0][...] = x
        grads = mm(x, w_out[...]).astype(bf16)
        columns_of = [masks[:, table : table + 1] for table in range(tables)]
        dq, dks, dvs = decoder_attend_back(grads, wide[...], logs[...], q[...], keys, values, columns_of)
        outs[1][...] = dq
        outs[2][...] = rows_sum(dq)
        partial = mm_t(dq, w_q[...]).astype(bf16)
        outs[3][...] = partial[: rows // 2]
        outs[4][...] = partial[rows // 2 :]
        total = 0.0
        for table in range(tables):
            outs[6 + table][...] = dks[table]
            outs[6 + tables + table][...] = dvs[table]
            total = total + rows_sum(dvs[table])
        outs[5][...] = total

    shapes = [(rows, width, bf16), (rows, columns, bf16), (1, columns, f32), (rows // 2, width, bf16), (rows // 2, width, bf16), (1, columns, f32)]
    shapes += [(slots, columns, bf16)] * (2 * tables)
    return call(
        kernel, (1,),
        [full(value.shape) for value in (*parts, w_out, wide, logs, q, masks, w_q, *keys, *values)],
        [full(shape[:2]) for shape in shapes], [shaped(*shape) for shape in shapes], [],
        cost(4 * rows * width * columns + 10 * rows * slots * columns, 8 * width * columns),
        *parts, w_out, wide, logs, q, masks, w_q, *keys, *values,
    )


def decoder_self_back(parts, w_out, wide, logs, q, k, v, masks, w_q, w_k, w_v):
    tables = masks.shape[0]
    rows, width = 2 * parts[0].shape[0], parts[0].shape[1]
    half = rows // (2 * tables)
    columns = w_q.shape[1]

    def kernel(own, other, w_out, wide, logs, q, k, v, masks, w_q, w_k, w_v, x_out, q_out, k_out, v_out, q_sum, v_sum, low, high):
        x = jnp.concatenate([own[...], other[...]], axis=0)
        x_out[...] = x
        grads = mm(x, w_out[...]).astype(bf16)
        keys, values = ([table_rows_of(value[...], table, tables, half) for table in range(tables)] for value in (k, v))
        dq, dks, dvs = decoder_attend_back(grads, wide[...], logs[...], q[...], keys, values, [masks[table] for table in range(tables)])
        dk, dv = in_frame(dks, half), in_frame(dvs, half)
        q_out[...], k_out[...], v_out[...] = dq, dk, dv
        q_sum[...], v_sum[...] = rows_sum(dq), rows_sum(dv)
        partial = (mm_t(dq, w_q[...]) + mm_t(dk, w_k[...]) + mm_t(dv, w_v[...])).astype(bf16)
        low[...] = partial[: rows // 2]
        high[...] = partial[rows // 2 :]

    shapes = [(rows, width, bf16)] + [(rows, columns, bf16)] * 3 + [(1, columns, f32)] * 2 + [(rows // 2, width, bf16)] * 2
    return call(
        kernel, (1,),
        [full(value.shape) for value in (*parts, w_out, wide, logs, q, k, v, masks, w_q, w_k, w_v)],
        [full(shape[:2]) for shape in shapes], [shaped(*shape) for shape in shapes], [],
        cost(12 * rows * width * columns, 8 * width * columns),
        *parts, w_out, wide, logs, q, k, v, masks, w_q, w_k, w_v,
    )


def per_device(
    table_input,
    target_input,
    cotangent,
    table_lengths,
    target_lengths,
    query_key,
    value_out,
    hidden_in,
    hidden_out,
    hidden_bias,
    vectors,
    cross_bias,
):
    sections = lax.axis_size("section")
    count = lax.axis_size("tensor")
    bits = axis_bits("tensor")
    rank = lax.axis_index("tensor")
    section = lax.axis_index("section")
    is_first = section == 0
    section_ref = section.reshape(1).astype(jnp.int32)
    in_line = lax.axis_size("dp") == CHUNKS
    place = lax.axis_index("dp")
    beyond = jnp.logical_and(in_line, place >= CHUNKS // 2).astype(jnp.int32)
    inner = jnp.where(in_line, ((place == 1) | (place == 2)).astype(jnp.int32), 1)
    line_ref = jnp.stack([beyond, inner])
    order_ref = (jnp.arange(CHUNKS, dtype=jnp.int32) + beyond * (CHUNKS // 2)) % CHUNKS
    place_ref = jnp.where(in_line, lax.axis_index("dp"), 0).reshape(1).astype(jnp.int32)
    tables, slots, width = table_input.shape
    targets = target_input.shape[1]
    columns = query_key.shape[3]
    rows = vectors[0]
    row = [rows[index : index + 1] for index in range(rows.shape[0])]
    head_rows = lax.dynamic_slice_in_dim(rows[0:3], rank * columns, columns, 1)
    no_bias = jnp.zeros((1, columns), f32)
    w_query, w_key, w_third_q = query_key[0, 0], query_key[0, 1], query_key[0, 2]
    w_value, w_out, w_third_v = value_out[0, 0], value_out[0, 1], value_out[0, 2]
    w_in, w_hidden_out = hidden_in[0], hidden_out[0]

    masks = [int(format(p, f"0{bits}b")[::-1], 2) for p in range(count)]
    owners = rank.astype(jnp.int32) ^ jnp.array(masks, jnp.int32)
    short = slots // (sections * count)
    row_index = (
        jnp.arange(sections)[None, :, None] * (count * short)
        + owners[:, None, None] * short
        + jnp.arange(short)[None, None, :]
    ).reshape(-1)
    table_valid = row_index[None, :] < table_lengths[:, None]
    table_mask = jnp.where(table_valid, 0.0, -1e30).astype(f32)

    cores = 2
    small = targets // (sections * count)
    core_order = (rank % cores) ^ jnp.arange(cores)
    half = targets // cores

    def target_frame(value):
        split = value.reshape(tables, sections, count // cores, cores, small, width)
        split = jnp.take(split, core_order, axis=3)
        return jnp.transpose(split, (3, 0, 2, 1, 4, 5)).reshape(cores, tables * half, width)

    target_index = (
        jnp.arange(sections)[None, None, :, None] * (count * small)
        + jnp.arange(count // cores)[None, :, None, None] * (cores * small)
        + core_order[:, None, None, None] * small
        + jnp.arange(small)[None, None, None, :]
    ).reshape(-1)
    target_rows = target_frame(target_input)
    grad_rows_half = target_frame(cotangent)[0]
    target_valid = target_index[None, :] < target_lengths[:, None]
    causal = (target_index[None, :] <= target_index[:, None])[None] & target_valid[:, None, :]

    causal_mask = jnp.where(causal, 0.0, -1e30).astype(f32)
    causal_back = jnp.swapaxes(causal_mask, 1, 2)

    encoder_kept, encoder_out = {}, {}
    cross, dec, grad_memory = {}, {}, {}
    w_cross_key = w_cross_value = b_cross_value = None
    order.last = None

    def encode(table):
        first_in, queries, keys, values, normed, raw = encoder_qkv(
            table_input, table, owners, row[9], row[10], w_query, w_key, w_value, head_rows[0:2], sections
        )
        yield "qkv"
        heads, wide, logs, low, high = encoder_attention(queries, keys, values, table_mask[table][None], w_out, count)
        sent = flip(high, 0)
        yield "attention"
        parts = reduce_rest(low, sent)
        yield "reduce"
        summed_one, middle, sent = norm_forward(normed, parts, row[3], row[5], row[6])
        started = gather_start(sent)
        yield "norm"
        parts = gather_rest(started)
        yield "gather"
        second_in, hidden, slope, low, high = ffn_forward(parts, w_in, hidden_bias, w_hidden_out)
        sent = flip(high, 0)
        yield "ffn"
        parts = reduce_rest(low, sent)
        yield "reduce two"
        summed_two, _, memory = norm_forward(middle, parts, row[4], row[7], row[8])
        encoder_kept[table] = (raw, first_in, queries, keys, values, heads, wide, logs, summed_one, second_in, hidden, slope, summed_two)
        memory = to_second(memory)
        yield "memory"
        started = gather_start(memory)
        yield "moved"
        yield "gather two"
        cross[table] = project_parts(gather_rest(started), [w_cross_key, w_cross_value], [no_bias, b_cross_value])
        yield "cross"

    def decode():
        dec["first"], q, k, v, heads, wide, logs, low, high = decoder_self(
            [target_rows[0], target_rows[1]], w_query, w_key, w_value, head_rows[0:2], causal_mask, w_out
        )
        dec["self"] = (q, k, v, heads, wide, logs)
        sent = flip(high, 0)
        yield "self"
        parts = half_rest(low, sent)
        yield "reduce"
        dec["one"], middle, sent = norm_forward(target_rows[0].astype(f32), parts, row[3], row[5], row[6])
        sent = gather_half(sent)
        yield "norm"
        keys, values = [cross[table][1] for table in range(tables)], [cross[table][2] for table in range(tables)]
        cross_in, q, heads, wide, logs, low, high = decoder_cross(
            sent, w_third_q, head_rows[2:3], keys, values, table_mask, w_third_v
        )
        parts = half_rest(low, flip(high, 0))
        three, later, sent = norm_forward(middle, parts, cross_bias[None], row[9], row[10])
        third_in, hidden, slope, low, high = ffn_forward(gather_half(sent), w_in, hidden_bias, w_hidden_out)
        parts = half_rest(low, flip(high, 0))
        two, _, dec["out"] = norm_forward(later, parts, row[4], row[7], row[8])
        grad_two, sent, dec["sums_two"] = norm_backward(two, row[7], [grad_rows_half])
        grad_two_rows, before_grad, low, high, dec["bias"] = ffn_backward(gather_half(sent), slope, w_in, w_hidden_out)
        parts = half_rest(low, flip(high, 0))
        grad_three, sent, dec["sums_three"] = norm_backward(three, row[9], [grad_two, *parts])
        grad_three_rows, dq, dec["third_sum"], low, high, third_bias, *rest = decoder_cross_back(
            gather_half(sent), w_third_v, wide, logs, q, keys, values, jnp.swapaxes(table_mask, 0, 1), w_third_q
        )
        dec["cross_rows"] = low, high
        dks, dvs = rest[:tables], rest[tables:]
        for table in range(tables):
            low, high = back_sum([dks[table], dvs[table]], [w_cross_key, w_cross_value], count)
            dec["memory", table] = low, flip(high, 0)
        dec["grad_three"] = grad_three
        dec["pairs"] = {"in": [(third_in, before_grad)], "out": [(grad_two_rows, hidden)]}
        yield "back"
        memory_rows = [cross[table][0] for table in range(tables)]
        arrived = weight_sum(memory_rows, dks), weight_sum(memory_rows, dvs)
        own = weight_sum([cross_in], [dq]), weight_sum([grad_three_rows], [heads])
        yield "thirds"
        arrived = [to_first(value) for value in gate(*arrived)]
        dec["third_bias"] = to_first(third_bias)
        yield "third send"
        first, *rest = pick_third(section_ref, place_ref, arrived, own)
        if in_line:
            sent = send_chunks(rest)
        yield "third pick"
        if in_line:
            total = sum_chunks(first, sent)
            sent = send_chunks([total] * (CHUNKS - 1))
            dec["thirds"] = [total, *sent]
        else:
            totals = lax.psum([first, *rest], "dp")
            dec["thirds"] = totals[:1] + totals[:0:-1]
        yield "third sum"
        dec["thirds"] = gate(*dec["thirds"])
        yield "third end"

    def memory_back(table):
        keep, sent = reduce_rest(*dec["memory", table])
        yield "reduce"
        grad_memory[table] = to_first(add_rows(keep, sent))
        yield "moved"

    def decode_rest():
        low, high = gate(*dec["cross_rows"])
        sent = flip(high, 0)
        yield "start"
        parts = half_rest(low, sent)
        yield "reduce"
        grad_one, sent, dec["sums_one"] = norm_backward(dec["one"], row[5], [dec["grad_three"], *parts])
        sent = gather_half(sent)
        yield "norm"
        q, k, v, heads, wide, logs = dec["self"]
        grad_one_rows, grad_q, grad_k, grad_v, dec["sum_q"], dec["sum_v"], low, high = decoder_self_back(
            sent, w_out, wide, logs, q, k, v, causal_back, w_query, w_key, w_value
        )
        first = dec["first"]
        dec["pairs"].update({"qk": [(first, grad_q), (first, grad_k)], "vo": [(first, grad_v), (grad_one_rows, heads)]})
        sent = flip(high, 0)
        yield "self"
        keep, sent = half_rest(low, sent)
        yield "reduce two"
        dec["target_grad"] = (grad_one + keep.astype(f32) + sent.astype(f32)).astype(bf16)

    def encode_back(table):
        (raw, first_in, queries, keys, values, heads, wide, logs, summed_one, second_in, hidden, slope, summed_two) = encoder_kept[table]
        grad_two, sent, sums_two = norm_backward(summed_two, row[7], [grad_memory[table]])
        started = gather_start(sent)
        yield "norm two"
        parts = gather_rest(started)
        pairs = encoder_out[table] = {"out": [(tuple(parts), hidden)]}
        yield "gather two"
        _, grad_before, low, high, bias = ffn_backward(parts, slope, w_in, w_hidden_out)
        pairs["in"] = [(second_in, grad_before)]
        sent = flip(high, 0)
        yield "ffn"
        parts = reduce_rest(low, sent)
        yield "reduce two"
        grad_one, sent, sums_one = norm_backward(summed_one, row[5], [grad_two, *parts])
        started = gather_start(sent)
        yield "norm one"
        yield "gather one"
        grad_one_rows, grad_q, grad_k, grad_v, sum_q, sum_v = encoder_attention_back(
            gather_rest(started), wide, logs, queries, keys, values, table_mask[table][:, None], w_out
        )
        pairs.update({"qk": [(first_in, grad_q), (first_in, grad_k)], "vo": [(first_in, grad_v), (grad_one_rows, heads)]})
        yield "attention"
        low, high = back_sum([grad_q, grad_k, grad_v], [w_query, w_key, w_value], count)
        sent = flip(high, 0)
        yield "back"
        parts = reduce_rest(low, sent)
        yield "reduce one"
        _, pairs["table_grad"], sums_zero = norm_backward(raw, row[9], [grad_one, *parts])
        pairs["sums"] = (sums_one, sums_two, sums_zero, sum_q, sum_v, bias)
        yield "norm zero"

    totals = {}

    def weights(name):
        totals[name] = []
        rows = weight_grad(section_ref, order_ref, [encoder_out[table][name] for table in range(tables)], dec["pairs"][name])
        yield from sum_line(rows, totals[name])
        if name in ("out", "in"):
            totals[name] = unite_one(line_ref, totals[name])
            yield "four"

    def cross_weights():
        nonlocal w_cross_key, w_cross_value, b_cross_value
        sent = gate(w_third_q, w_third_v, head_rows[2:3])
        w_cross_key, w_cross_value, b_cross_value = (to_second(value) for value in sent)
        yield "send"
        w_cross_key, w_cross_value, b_cross_value = gate(w_cross_key, w_cross_value, b_cross_value)
        yield "gate"

    parts = {"d": decode(), "g": cross_weights(), "r": decode_rest()}
    for table in range(tables):
        parts[f"e{table}"] = encode(table)
        parts[f"m{table}"] = memory_back(table)
        parts[f"b{table}"] = encode_back(table)
    for name in ("out", "in", "qk", "vo"):
        parts[name] = weights(name)
    for name, label in ORDER:
        for said in parts[name]:
            if said == label:
                break
    for part in parts.values():
        for _ in part:
            pass

    table_grads = [encoder_out[table]["table_grad"] for table in range(tables)]
    decoded, target_grad = dec["out"], dec["target_grad"]
    total_out, total_in = totals["out"], totals["in"]

    bundle = vector_rows(
        section_ref,
        rank.reshape(1).astype(jnp.int32),
        [encoder_out[table]["sums"] for table in range(tables)],
        dec["third_bias"],
        [dec[name] for name in ("sums_one", "sums_two", "sums_three", "sum_q", "sum_v", "third_sum", "bias")],
        cores / count,
    )
    bundle = sum_over(bundle, "dp")
    query_key_grad, value_out_grad = unite(place_ref, line_ref, totals["qk"], totals["vo"], dec["thirds"])
    bias_sum = bundle[12:13, : w_in.shape[1]]
    bundle = sum_over(bundle, "tensor")
    vector_total = bundle[:11]
    cross_total = bundle[11] + lax.ppermute(bundle[11], "section", [(0, 1), (1, 0)])

    table_grads = jnp.stack(table_grads).reshape(tables, sections, short, width)
    moved_up = lax.ppermute(table_grads[:, 1], "section", [(0, 1)])
    table_out = jnp.where(is_first, table_grads[:, 0], moved_up)
    own = lax.dynamic_slice_in_dim(
        jnp.stack([decoded, target_grad]).reshape(2, tables, count // cores, sections, small, width),
        rank // cores,
        1,
        2,
    )[:, :, 0]
    moved_down = lax.ppermute(own[:, :, 0], "section", [(1, 0)])
    small_out = jnp.where(is_first, moved_down, own[:, :, 1])
    return (
        small_out[0],
        table_out,
        small_out[1],
        query_key_grad[None],
        value_out_grad[None],
        total_in[None],
        total_out[None],
        bias_sum,
        vector_total[None],
        cross_total,
    )


def solution(mesh):
    in_specs = (
        P("dp", None, None),
        P("dp", None, None),
        P("dp", None, None),
        P("dp"),
        P("dp"),
        P("section", None, None, "tensor"),
        P("section", None, None, "tensor"),
        P("section", None, "tensor"),
        P("section", None, "tensor"),
        P("section", "tensor"),
        P("section", None, None),
        P(),
    )
    out_specs = (
        P("dp", ("section", "tensor"), None),
        P("dp", ("section", "tensor"), None),
        P("dp", ("section", "tensor"), None),
        P("section", None, None, "tensor"),
        P("section", None, None, "tensor"),
        P("section", None, "tensor"),
        P("section", None, "tensor"),
        P("section", "tensor"),
        P("section", None, None),
        P(),
    )
    return jax.shard_map(
        per_device, mesh=mesh, in_specs=in_specs, out_specs=out_specs, check_vma=False
    )
```

```python
import jax
import jax.numpy as jnp
from jax import lax
from jax.experimental import pallas as pl
from jax.experimental.pallas import tpu as pltpu
from jax.sharding import PartitionSpec as P

HEAD = 64
SCALING = HEAD ** (-0.5)
EPSILON = 1e-05

bf16 = jnp.bfloat16
f32 = jnp.float32


def mm(a, b):
    return lax.dot_general(a, b, (((1,), (0,)), ((), ())), preferred_element_type=f32)


def mm_t(a, b):
    return lax.dot_general(a, b, (((1,), (1,)), ((), ())), preferred_element_type=f32)


def t_mm(a, b):
    return lax.dot_general(a, b, (((0,), (0,)), ((), ())), preferred_element_type=f32)


def norm_stats(summed):
    centered = summed - jnp.mean(summed, axis=-1, keepdims=True)
    spread = jnp.mean(centered * centered, axis=-1, keepdims=True)
    scale = lax.rsqrt(spread + EPSILON)
    return centered * scale, scale


def gelu_pair(before):
    cumulative = 0.5 * (1.0 + lax.erf(before * (0.5 ** 0.5)))
    density = jnp.exp(-0.5 * before * before) * 0.3989422804014327
    return before * cumulative, cumulative + before * density


def shaped(rows, width, dtype=bf16):
    return jax.ShapeDtypeStruct((rows, width), dtype)


def full(shape):
    return pl.BlockSpec(shape, lambda *_: (0,) * len(shape))


def turned(steps):
    return lambda i, *_: ((i + steps // 2) % steps, 0)


def low_high(rows, width, steps):
    return [
        pl.BlockSpec((rows, width), lambda i, *_: (jnp.maximum(i - steps // 2, 0), 0)),
        pl.BlockSpec((rows, width), lambda i, *_: (jnp.minimum(i, steps // 2 - 1), 0)),
    ]


def put_low_high(value, low, high):
    first = pl.program_id(0) < pl.num_programs(0) // 2

    @pl.when(first)
    def _():
        high[...] = value

    @pl.when(jnp.logical_not(first))
    def _():
        low[...] = value


def pick_block(parts, held):
    steps = len(parts)
    at = (pl.program_id(0) + steps // 2) % steps
    for index, part in enumerate(parts):
        @pl.when(at == index)
        def _(part=part):
            held[...] = part[...]
    return held[...]


def cost(flops, moved, exps=0):
    return pl.CostEstimate(flops=int(flops), bytes_accessed=int(moved), transcendentals=int(exps))


ORDER = (
    ("g", "send"),
    ("e0", "qkv"),
    ("e0", "attention"),
    ("g", "gate"),
    ("e1", "qkv"),
    ("e0", "reduce"),
    ("e1", "attention"),
    ("e0", "norm"),
    ("e1", "reduce"),
    ("d", "self"),
    ("d", "reduce"),
    ("e0", "ffn"),
    ("e1", "norm"),
    ("d", "norm"),
    ("e0", "reduce two"),
    ("e1", "ffn"),
    ("e0", "memory"),
    ("e1", "reduce two"),
    ("e1", "memory"),
    ("e0", "cross"),
    ("e1", "cross"),
    ("d", "back"),
    ("m0", "reduce"),
    ("m1", "reduce"),
    ("d", "thirds"),
    ("m0", "moved"),
    ("m1", "moved"),
    ("b0", "norm two"),
    ("b1", "norm two"),
    ("r", "start"),
    ("d", "third send"),
    ("b0", "ffn"),
    ("r", "reduce"),
    ("b0", "reduce two"),
    ("d", "third pick"),
    ("b1", "ffn"),
    ("b0", "norm one"),
    ("b1", "reduce two"),
    ("out", "made"),
    ("d", "third sum"),
    ("in", "made"),
    ("r", "norm"),
    ("b0", "attention"),
    ("b1", "norm one"),
    ("r", "self"),
    ("b0", "back"),
    ("r", "reduce two"),
    ("b0", "reduce one"),
    ("out", "one"),
    ("b1", "attention"),
    ("out", "two"),
    ("qk", "made"),
    ("vo", "made"),
    ("in", "one"),
    ("b1", "back"),
    ("b0", "norm zero"),
    ("out", "three"),
    ("b1", "reduce one"),
    ("in", "two"),
    ("b1", "norm zero"),
    ("d", "third end"),
    ("qk", "one"),
    ("vo", "one"),
    ("in", "three"),
    ("out", "four"),
    ("qk", "two"),
    ("vo", "two"),
    ("in", "four"),
    ("qk", "three"),
    ("vo", "three"),
)


class Order:
    def __init__(self):
        self.last = None


order = Order()


def call(kernel, grid, in_specs, out_specs, out_shape, scratch, estimate, *args, prefetch=()):
    count = len(prefetch) + len(args)
    after = [] if order.last is None else [order.last]

    def ordered(*refs):
        kernel(*refs[:count], *refs[count + len(after) :])

    grid_spec = pltpu.PrefetchScalarGridSpec(
        num_scalar_prefetch=len(prefetch),
        grid=grid,
        in_specs=list(in_specs) + [pl.BlockSpec(memory_space=pl.ANY)] * len(after),
        out_specs=out_specs,
        scratch_shapes=scratch,
    )
    results = pl.pallas_call(
        ordered,
        grid_spec=grid_spec,
        out_shape=out_shape,
        compiler_params=pltpu.CompilerParams(vmem_limit_bytes=48 * 1024 * 1024),
        cost_estimate=estimate,
        name=kernel.__qualname__.split(".")[0],
    )(*prefetch, *args, *after)
    order.last = min(results, key=lambda result: result.size) if isinstance(results, (list, tuple)) else results
    return results


def gate(*values, behind=()):
    count = len(values)
    after = ([] if order.last is None else [order.last]) + list(behind)
    results = pl.pallas_call(
        lambda *refs: None,
        in_specs=[pl.BlockSpec(memory_space=pl.ANY)] * (count + len(after)),
        out_specs=[pl.BlockSpec(memory_space=pl.ANY)] * count,
        out_shape=[jax.ShapeDtypeStruct(value.shape, value.dtype) for value in values],
        input_output_aliases={index: index for index in range(count)},
        cost_estimate=cost(0, 0),
        name="gate",
    )(*values, *after)
    order.last = results[0]
    return results if count > 1 else results[0]


def norm_kernel(residual, keep, sent, bias, gain, shift, summed_out, wide_out, out):
    summed = residual[...] + (keep[...].astype(f32) + sent[...].astype(f32)) + bias[...]
    normed = norm_stats(summed)[0] * gain[...] + shift[...]
    summed_out[...] = summed
    wide_out[...] = normed
    out[...] = normed.astype(bf16)


def norm_forward(residual, parts, bias, gain, shift):
    rows, width = residual.shape
    block, row = full((rows, width)), full((1, width))
    return call(
        norm_kernel, (1,), [block] * 3 + [row] * 3, [block] * 3,
        [shaped(rows, width, f32)] * 2 + [shaped(rows, width)], [],
        cost(12 * rows * width, 18 * rows * width),
        residual, *parts, bias, gain, shift,
    )


def norm_back_kernel(count, *refs):
    grads, (summed, gain, wide_out, out, sums) = refs[:count], refs[count:]
    gradient = grads[0][...].astype(f32)
    for grad in grads[1:]:
        gradient = gradient + grad[...].astype(f32)
    unit, scale = norm_stats(summed[...].astype(f32))
    scaled = gradient * gain[...]
    inner = scaled - jnp.mean(scaled, axis=-1, keepdims=True)
    inner = (inner - unit * jnp.mean(scaled * unit, axis=-1, keepdims=True)) * scale
    wide_out[...] = inner
    out[...] = inner.astype(bf16)
    sums[...] = jnp.concatenate(
        [
            jnp.sum(gradient * unit, axis=0, keepdims=True),
            jnp.sum(gradient, axis=0, keepdims=True),
            jnp.sum(inner, axis=0, keepdims=True),
            jnp.zeros((5, inner.shape[1]), f32),
        ]
    )


def norm_backward(summed, gain, grads):
    rows, width = summed.shape
    block, row = full((rows, width)), full((1, width))

    def kernel(*refs):
        norm_back_kernel(len(grads), *refs)

    return call(
        kernel, (1,), [block] * (len(grads) + 1) + [row], [block] * 2 + [full((8, width))],
        [shaped(rows, width, f32), shaped(rows, width), shaped(8, width, f32)], [],
        cost(20 * rows * width, 18 * rows * width),
        *grads, summed, gain,
    )


def qkv_kernel(sections, owners, *refs):
    parts = refs[:sections]
    gain, shift, w_q, w_k, w_v, bias, x_out, q_out, k_out, v_out, own_norm, own_raw = refs[sections:]
    raw = jnp.concatenate([part[...] for part in parts], axis=0)
    normed = norm_stats(raw.astype(f32))[0] * gain[...] + shift[...]
    x = normed.astype(bf16)
    x_out[...] = x
    q_out[...] = (mm(x, w_q[...]) + bias[0:1]).astype(bf16)
    k_out[...] = mm(x, w_k[...]).astype(bf16)
    v_out[...] = (mm(x, w_v[...]) + bias[1:2]).astype(bf16)

    @pl.when(pl.program_id(0) == 0)
    def _():
        own_norm[...] = normed
        own_raw[...] = raw


def encoder_qkv(table_rows, table, owners, gain, shift, w_q, w_k, w_v, bias, sections):
    slots, width = table_rows.shape[1:]
    count = owners.shape[0]
    short = slots // (sections * count)
    share = sections * short
    columns = w_q.shape[1]

    def part_spec(s):
        return pl.BlockSpec((None, short, width), lambda i, order: (table, s * count + order[i], 0))

    def block(columns):
        return pl.BlockSpec((share, columns), lambda i, order: (i, 0))

    def kernel(*refs):
        qkv_kernel(sections, *refs)

    return call(
        kernel, (count,),
        [part_spec(s) for s in range(sections)] + [full((1, width))] * 2 + [full((width, columns))] * 3 + [full(bias.shape)],
        [block(width)] + [block(columns)] * 3 + [full((share, width))] * 2,
        [shaped(slots, width)] + [shaped(slots, columns)] * 3 + [shaped(share, width, f32), shaped(share, width)],
        [],
        cost(6 * slots * width * columns, 8 * slots * width),
        *([table_rows] * sections), gain, shift, w_q, w_k, w_v, bias,
        prefetch=[owners],
    )


def pair_mask(head):
    return (lax.broadcasted_iota(jnp.int32, (1, 128), 1) // HEAD) == head


def attention_rows(q_all, k_all, v_all, mask):
    rows, columns = q_all.shape
    lanes = lax.broadcasted_iota(jnp.int32, (rows, 128), 1)
    logs = jnp.zeros((rows, 128), f32)
    parts = []
    for pair in range(columns // 128):
        at = slice(pair * 128, pair * 128 + 128)
        q = q_all[:, at] * jnp.asarray(SCALING, bf16)
        k, v = k_all[:, at], v_all[:, at]
        outs = []
        for head in range(2):
            scores = mm_t(jnp.where(pair_mask(head), q, jnp.zeros_like(q)), k) + mask
            largest = jnp.max(scores, axis=-1, keepdims=True)
            exponent = jnp.exp(scores - largest)
            total = jnp.sum(exponent, axis=-1, keepdims=True)
            outs.append(mm(exponent.astype(bf16), v) / total)
            logs = jnp.where(lanes == pair * 2 + head, largest + jnp.log(total), logs)
        parts.append(jnp.where(pair_mask(0), outs[0], outs[1]))
    return jnp.concatenate(parts, axis=1), jnp.transpose(logs)


def attention_kernel(q_ref, k_ref, v_ref, mask_ref, w_out, heads_out, wide_out, log_out, low, high):
    wide, logs = attention_rows(q_ref[...], k_ref, v_ref, mask_ref[...])
    heads = wide.astype(bf16)
    wide_out[...] = wide
    heads_out[...] = heads
    log_out[...] = logs[: log_out.shape[0]]
    put_low_high(mm_t(heads, w_out[...]).astype(bf16), low, high)


def encoder_attention(queries, keys, values, mask, w_out, steps):
    slots, columns = queries.shape
    width = w_out.shape[0]
    rows = slots // steps
    block = pl.BlockSpec((rows, columns), turned(steps))
    return call(
        attention_kernel, (steps,),
        [block, full((slots, columns)), full((slots, columns)), full((1, slots)), full((width, columns))],
        [block, block, pl.BlockSpec((8, rows), lambda i: (0, (i + steps // 2) % steps))] + low_high(rows, width, steps),
        [shaped(slots, columns), shaped(slots, columns, f32), shaped(8, slots, f32)] + [shaped(slots // 2, width)] * 2,
        [],
        cost(8 * slots * slots * columns, 8 * slots * columns + 2 * slots * width, slots * slots * columns // HEAD),
        queries, keys, values, mask, w_out,
    )


def attention_back_rows(grads, wide, logs, q_all, k_all, v_all, mask, add):
    inner = jnp.transpose(grads.astype(f32) * wide)
    sub = lax.broadcasted_iota(jnp.int32, (128, 1), 0) // HEAD
    parts = []
    for pair in range(grads.shape[1] // 128):
        at = slice(pair * 128, pair * 128 + 128)
        q = q_all[:, at] * jnp.asarray(SCALING, bf16)
        k, v, g = k_all[:, at], v_all[:, at], grads[:, at]
        dk, dv, dq = 0.0, 0.0, []
        for head in range(2):
            keep = pair_mask(head)
            q_one = jnp.where(keep, q, jnp.zeros_like(q))
            g_one = jnp.where(keep, g, jnp.zeros_like(g))
            at_head = pair * 2 + head
            probability = jnp.exp((mm_t(k, q_one) + mask) - logs[at_head : at_head + 1, :])
            dv = dv + mm(probability.astype(bf16), g_one)
            delta = jnp.sum(inner[at_head * HEAD : (at_head + 1) * HEAD], axis=0, keepdims=True)
            scores_grad = (probability * (mm_t(v, g_one) - delta)).astype(bf16)
            dk = dk + mm(scores_grad, q_one)
            dq.append(t_mm(k, scores_grad))
        add(at, dk, dv)
        parts.append(jnp.transpose(jnp.where(sub == 0, dq[0], dq[1]) * SCALING))
    return jnp.concatenate(parts, axis=1).astype(bf16)


def attention_back_kernel(steps, *refs):
    parts = refs[:steps]
    (wide_ref, log_ref, q_ref, k_ref, v_ref, mask_ref, w_out, rows_out, dq_out, dk_out, dv_out, q_sum, v_sum, held, dk_sum, dv_sum) = refs[steps:]
    step = pl.program_id(0)
    grad_rows = pick_block(parts, held)
    rows_out[...] = grad_rows
    grads = mm(grad_rows, w_out[...]).astype(bf16)

    @pl.when(step == 0)
    def _():
        dk_sum[...] = jnp.zeros_like(dk_sum)
        dv_sum[...] = jnp.zeros_like(dv_sum)
        q_sum[...] = jnp.zeros_like(q_sum)

    def add(at, dk, dv):
        dk_sum[:, at] += dk
        dv_sum[:, at] += dv

    dq = attention_back_rows(grads, wide_ref[...], log_ref, q_ref[...], k_ref, v_ref, mask_ref[...], add)
    dq_out[...] = dq
    q_sum[...] += jnp.sum(dq.astype(f32), axis=0, keepdims=True)

    @pl.when(step == steps - 1)
    def _():
        dk_out[...] = dk_sum[...].astype(bf16)
        dv = dv_sum[...].astype(bf16)
        dv_out[...] = dv
        v_sum[...] = jnp.sum(dv.astype(f32), axis=0, keepdims=True)


def encoder_attention_back(grad_parts, wide, logs, queries, keys, values, mask, w_out):
    slots, columns = queries.shape
    width = w_out.shape[0]
    steps = len(grad_parts)
    rows = slots // steps
    whole, row = full((slots, columns)), full((1, columns))
    block = pl.BlockSpec((rows, columns), turned(steps))

    def kernel(*refs):
        attention_back_kernel(steps, *refs)

    return call(
        kernel, (steps,),
        [full((rows, width))] * steps
        + [block, pl.BlockSpec((8, rows), lambda i: (0, (i + steps // 2) % steps)), block, whole, whole, full((slots, 1)), full((width, columns))],
        [pl.BlockSpec((rows, width), turned(steps)), block, whole, whole, row, row],
        [shaped(slots, width)] + [shaped(slots, columns)] * 3 + [shaped(1, columns, f32)] * 2,
        [pltpu.VMEM((rows, width), bf16)] + [pltpu.VMEM((slots, columns), f32)] * 2,
        cost(20 * slots * slots * columns, 16 * slots * columns + 2 * slots * width, slots * slots * columns // HEAD),
        *grad_parts, wide, logs, queries, keys, values, mask, w_out,
    )


def ffn_kernel(steps, *refs):
    parts, (w_in, bias, w_out, x_out, hidden_out, slope_out, low, high, held) = refs[:steps], refs[steps:]
    x = pick_block(parts, held)
    x_out[...] = x
    hidden, slope = gelu_pair(mm(x, w_in[...]) + bias[...])
    hidden = hidden.astype(bf16)
    hidden_out[...] = hidden
    slope_out[...] = slope.astype(bf16)
    put_low_high(mm_t(hidden, w_out[...]).astype(bf16), low, high)


def ffn_forward(parts, w_in, bias, w_out):
    steps = len(parts)
    rows, width = parts[0].shape
    slots = rows * steps
    units = w_in.shape[1]
    block = pl.BlockSpec((rows, units), turned(steps))

    def kernel(*refs):
        ffn_kernel(steps, *refs)

    return call(
        kernel, (steps,),
        [full((rows, width))] * steps + [full((width, units)), full((1, units)), full((width, units))],
        [pl.BlockSpec((rows, width), turned(steps)), block, block] + low_high(rows, width, steps),
        [shaped(slots, width)] + [shaped(slots, units)] * 2 + [shaped(slots // 2, width)] * 2,
        [pltpu.VMEM((rows, width), bf16)],
        cost(4 * slots * width * units, 8 * slots * units + 4 * units * width, 2 * slots * units),
        *parts, w_in, bias, w_out,
    )


def ffn_back_kernel(steps, *refs):
    parts, (slope, w_in, w_out, x_out, before_out, low, high, bias_out, held) = refs[:steps], refs[steps:]
    x = pick_block(parts, held)
    x_out[...] = x
    before = (mm(x, w_out[...]) * slope[...].astype(f32)).astype(bf16)
    before_out[...] = before

    @pl.when(pl.program_id(0) == 0)
    def _():
        bias_out[...] = jnp.zeros_like(bias_out)

    bias_out[...] += jnp.sum(before.astype(f32), axis=0, keepdims=True)
    put_low_high(mm_t(before, w_in[...]).astype(bf16), low, high)


def ffn_backward(parts, slope, w_in, w_out):
    steps = len(parts)
    rows, width = parts[0].shape
    slots = rows * steps
    units = w_in.shape[1]
    block = pl.BlockSpec((rows, units), turned(steps))

    def kernel(*refs):
        ffn_back_kernel(steps, *refs)

    return call(
        kernel, (steps,),
        [full((rows, width))] * steps + [block, full((width, units)), full((width, units))],
        [pl.BlockSpec((rows, width), turned(steps)), block] + low_high(rows, width, steps) + [full((1, units))],
        [shaped(slots, width), shaped(slots, units)] + [shaped(slots // 2, width)] * 2 + [shaped(1, units, f32)],
        [pltpu.VMEM((rows, width), bf16)],
        cost(4 * slots * width * units, 6 * slots * units + 4 * units * width),
        *parts, slope, w_in, w_out,
    )


def back_sum(values, matrices, steps):
    slots, columns = values[0].shape
    width = matrices[0].shape[0]
    rows = slots // steps
    count = len(values)

    def kernel(*refs):
        total = 0.0
        for value, matrix in zip(refs[:count], refs[count : 2 * count]):
            total = total + mm_t(value[...], matrix[...])
        put_low_high(total.astype(bf16), *refs[2 * count :])

    return call(
        kernel, (steps,),
        [pl.BlockSpec((rows, columns), turned(steps))] * count + [full((width, columns))] * count,
        low_high(rows, width, steps),
        [shaped(slots // 2, width)] * 2, [],
        cost(2 * count * slots * width * columns, 2 * slots * width),
        *values, *matrices,
    )


def project_parts(parts, matrices, biases):
    steps = len(parts)
    rows, width = parts[0].shape
    slots = rows * steps
    columns = matrices[0].shape[1]
    count = len(matrices)

    def kernel(*refs):
        held = refs[-1]
        x = pick_block(refs[:steps], held)
        inner = refs[steps:-1]
        inner[2 * count][...] = x
        for index in range(count):
            inner[2 * count + 1 + index][...] = (mm(x, inner[index][...]) + inner[count + index][...]).astype(bf16)

    return call(
        kernel, (steps,),
        [full((rows, width))] * steps + [full((width, columns))] * count + [full((1, columns))] * count,
        [pl.BlockSpec((rows, width), turned(steps))] + [pl.BlockSpec((rows, columns), turned(steps))] * count,
        [shaped(slots, width)] + [shaped(slots, columns)] * count,
        [pltpu.VMEM((rows, width), bf16)],
        cost(2 * count * slots * width * columns, 4 * slots * width),
        *parts, *matrices, *biases,
    )


CHUNKS = 4


def weight_grad(section, order_ref, enc_pairs, dec_pairs):
    pairs = [(x if isinstance(x, tuple) else (x,), g) for one in (*enc_pairs, dec_pairs) for x, g in one]
    width = pairs[0][0][0].shape[1]
    chunk = width // CHUNKS
    tables, count = len(enc_pairs), len(dec_pairs)
    total_columns = sum(g.shape[1] for _, g in dec_pairs)
    starts, in_specs, args = [], [], []
    for x, g in pairs:
        starts.append(len(args))
        in_specs += [pl.BlockSpec((part.shape[0], chunk), lambda i, s, at: (0, at[i])) for part in x] + [full(g.shape)]
        args += [*x, g]

    def kernel(at, order_at, *refs):
        out = refs[-1]

        def one_product(index):
            start, blocks = starts[index], len(pairs[index][0])
            x = jnp.concatenate([ref[...] for ref in refs[start : start + blocks]], axis=0) if blocks > 1 else refs[start][...]
            return t_mm(x, refs[start + blocks][...])

        def product(index):
            return jnp.concatenate([one_product(index * count + one) for one in range(count)], axis=1)

        @pl.when(at[0] == 0)
        def _():
            total = 0.0
            for table in range(tables):
                total = total + product(table)
            out[...] = total.astype(bf16)

        @pl.when(at[0] != 0)
        def _():
            out[...] = product(tables).astype(bf16)

    rows = sum(g.shape[0] for _, g in pairs) // count
    return call(
        kernel, (CHUNKS,), in_specs,
        pl.BlockSpec((None, chunk, total_columns), lambda i, *_: (i, 0, 0)),
        jax.ShapeDtypeStruct((CHUNKS, chunk, total_columns), bf16), [],
        cost(2 * rows * width * total_columns, 2 * rows * (width + total_columns)),
        *args,
        prefetch=[section, order_ref],
    )


def sum_line(rows, parts):
    half = (CHUNKS // 2, *rows.shape[1:])
    if lax.axis_size("dp") != CHUNKS:
        rows = lax.psum(rows, "dp")
        parts.extend([rows[: CHUNKS // 2], rows[CHUNKS // 2 :]] * 2)
        return
    inward, across, outward = [(0, 1), (3, 2)], [(1, 2), (2, 1)], [(1, 0), (2, 3)]
    sent = lax.ppermute(rows, "dp", inward)
    yield "made"

    def block(shape):
        return pl.BlockSpec(shape, lambda *_: (0, 0, 0))

    def add_side(rows_ref, sent_ref, own, other):
        for index in range(CHUNKS):
            total = (rows_ref[index].astype(f32) + sent_ref[index].astype(f32)).astype(bf16)
            (own if index < CHUNKS // 2 else other)[index % (CHUNKS // 2)] = total

    own, other = call(
        add_side, (1,), [block(rows.shape)] * 2, [block(half)] * 2, [jax.ShapeDtypeStruct(half, bf16)] * 2, [],
        cost(0, 6 * rows.size), rows, sent,
    )
    sent = lax.ppermute(other, "dp", across)
    yield "one"

    def add_across(own_ref, sent_ref, out):
        for index in range(CHUNKS // 2):
            out[index] = (own_ref[index].astype(f32) + sent_ref[index].astype(f32)).astype(bf16)

    total = call(
        add_across, (1,), [block(half)] * 2, block(half), jax.ShapeDtypeStruct(half, bf16), [], cost(0, 3 * rows.size), own, sent
    )
    crossed = lax.ppermute(total, "dp", across)
    first = lax.ppermute(total, "dp", outward)
    yield "two"
    crossed, first = gate(crossed, first)
    second = lax.ppermute(crossed, "dp", outward)
    parts.extend([total, crossed, first, second])
    yield "three"


def put_chunk(line, parts, put):
    step = pl.program_id(0)
    other = (step // (CHUNKS // 2)) ^ line[0]
    for index, part in enumerate(parts):
        @pl.when(jnp.logical_and(other == index % 2, line[1] == 1 - index // 2))
        def _(part=part):
            put(part[step % (CHUNKS // 2)])


def unite_one(line, parts):
    half, chunk, columns = parts[0].shape

    def kernel(line_at, *refs):
        def put(value):
            refs[-1][...] = value.astype(f32)

        put_chunk(line_at, refs[:-1], put)

    return call(
        kernel, (CHUNKS,), [pl.BlockSpec(parts[0].shape, lambda *_: (0, 0, 0))] * 4,
        pl.BlockSpec((chunk, columns), lambda i, *_: (i, 0)),
        shaped(CHUNKS * chunk, columns, f32), [], cost(0, 24 * chunk * columns), *parts,
        prefetch=[line],
    )


def pick_third(section, place, arrived, own):
    width, columns = own[0].shape
    rows = width // CHUNKS

    def kernel(at, place_at, *refs):
        turn = (pl.program_id(0) - place_at[0]) % CHUNKS
        first = at[0] == 0
        value = jnp.concatenate([jnp.where(first, a[...], b[...]) for a, b in zip(refs[:2], refs[2:4])], axis=1)
        for index in range(CHUNKS):
            @pl.when(turn == index)
            def _(index=index):
                refs[4 + index][...] = value

    block = pl.BlockSpec((rows, columns), lambda i, *_: (i, 0))
    return call(
        kernel, (CHUNKS,), [block] * 4, [full((rows, 2 * columns))] * CHUNKS, [shaped(rows, 2 * columns)] * CHUNKS, [],
        cost(0, 8 * width * columns), *arrived, *own,
        prefetch=[section, place],
    )


def send_chunks(chunks):
    return [lax.ppermute(chunk, "dp", [(i, (i + s + 1) % CHUNKS) for i in range(CHUNKS)]) for s, chunk in enumerate(chunks)]


def sum_chunks(own, sent):
    def kernel(*refs):
        total = refs[0][...].astype(f32)
        for ref in refs[1:-1]:
            total = total + ref[...].astype(f32)
        refs[-1][...] = total.astype(bf16)

    return call(
        kernel, (1,), [full(own.shape)] * CHUNKS, full(own.shape), shaped(*own.shape), [], cost(0, 10 * own.size), own, *sent
    )


def unite(place, line, qk, vo, thirds):
    rows, columns = qk[0].shape[1], qk[0].shape[2] // 2

    def kernel(place_at, line_at, *refs):
        qk, vo, chunks, (first, second) = refs[:4], refs[4:8], refs[8 : 8 + CHUNKS], refs[8 + CHUNKS :]
        for parts, out in ((qk, first), (vo, second)):
            def put(value, out=out):
                out[0] = value[:, :columns].astype(f32)
                out[1] = value[:, columns:].astype(f32)

            put_chunk(line_at, parts, put)
        turn = (place_at[0] - pl.program_id(0)) % CHUNKS
        for index in range(CHUNKS):
            @pl.when(turn == index)
            def _(index=index):
                first[2] = chunks[index][:, :columns].astype(f32)
                second[2] = chunks[index][:, columns:].astype(f32)

    stacked = pl.BlockSpec((3, rows, columns), lambda i, *_: (0, i, 0))
    return call(
        kernel, (CHUNKS,),
        [pl.BlockSpec(qk[0].shape, lambda *_: (0, 0, 0))] * 8 + [full((rows, 2 * columns))] * CHUNKS, [stacked] * 2,
        [jax.ShapeDtypeStruct((3, CHUNKS * rows, columns), f32)] * 2, [],
        cost(0, 36 * CHUNKS * rows * columns), *qk, *vo, *thirds,
        prefetch=[place, line],
    )


def vector_rows(section, rank, encoder, third_bias, decoder, factor):
    width = decoder[0].shape[1]
    columns, units = decoder[3].shape[1], decoder[6].shape[1]
    args = [value for one in encoder for value in one] + [third_bias, *decoder]
    tables, each = len(encoder), len(encoder[0])

    def kernel(at, rank_at, *refs):
        out = refs[-1]
        out[...] = jnp.zeros_like(out)

        def put(one, two, last, heads, bias, scale):
            picked = [one[2:3], two[2:3], one[0:1], one[1:2], two[0:1], two[1:2], last[0:1], last[1:2]]
            for index, value in enumerate(picked):
                out[3 + index : 4 + index, :] = value * scale
            out[12:13, :units] = bias
            for place in range(width // columns):
                @pl.when(rank_at[0] == place)
                def _(place=place):
                    for index, value in enumerate(heads):
                        out[index : index + 1, place * columns : (place + 1) * columns] = value

        @pl.when(at[0] == 0)
        def _():
            one, two, last, q, v, bias = (sum(refs[table * each + index][...] for table in range(tables)) for index in range(each))
            put(one, two, last, (q, v, refs[tables * each][...]), bias, 1.0)

        @pl.when(at[0] != 0)
        def _():
            one, two, last, q, v, third, bias = (ref[...] for ref in refs[tables * each + 1 : -1])
            put(one, two, last, (q, v, third), bias, factor)
            out[11:12, :] = last[2:3] * factor

    return call(
        kernel, (1,), [full(value.shape) for value in args], full((16, width)), shaped(16, width, f32), [], cost(0, 200 * width),
        *args, prefetch=[section, rank],
    )


def weight_sum(xs, gs):
    count = len(xs)
    width, columns = xs[0].shape[1], gs[0].shape[1]

    def kernel(*refs):
        total = t_mm(refs[0][...], refs[count][...])
        for index in range(1, count):
            total = total + t_mm(refs[index][...], refs[count + index][...])
        refs[-1][...] = total.astype(bf16)

    rows = sum(x.shape[0] for x in xs)
    return call(
        kernel, (1,), [full(value.shape) for value in (*xs, *gs)], full((width, columns)), shaped(width, columns), [],
        cost(2 * rows * width * columns, 2 * rows * (width + columns)),
        *xs, *gs,
    )


def add_halves(low, sent):
    rows, width = low.shape[0] // 2, low.shape[1]

    def kernel(low_ref, sent_ref, low_out, high_out):
        total = (low_ref[...].astype(f32) + sent_ref[...].astype(f32)).astype(bf16)
        low_out[...] = total[:rows]
        high_out[...] = total[rows:]

    return call(
        kernel, (1,), [full((2 * rows, width))] * 2, [full((rows, width))] * 2, [shaped(rows, width)] * 2, [],
        cost(2 * rows * width, 12 * rows * width), low, sent,
    )


def add_rows(low, sent):
    rows, width = low.shape

    def kernel(low_ref, sent_ref, out):
        out[...] = (low_ref[...].astype(f32) + sent_ref[...].astype(f32)).astype(bf16)

    return call(
        kernel, (1,), [full((rows, width))] * 2, full((rows, width)), shaped(rows, width), [],
        cost(rows * width, 6 * rows * width), low, sent,
    )


def flip(value, bit, axis="tensor"):
    count = lax.axis_size(axis)
    return lax.ppermute(value, axis, [(i, i ^ (1 << bit)) for i in range(count)])


def axis_bits(axis):
    return lax.axis_size(axis).bit_length() - 1


def reduce_rest(low, sent):
    for bit in range(1, axis_bits("tensor")):
        low, high = add_halves(low, sent)
        sent = flip(high, bit)
    return low, sent


def gather_start(share):
    return [share] + [flip(share, bit) for bit in reversed(range(axis_bits("tensor")))]


def gather_rest(started):
    parts, first = [started[0]], started[1:]
    for index, bit in enumerate(reversed(range(axis_bits("tensor")))):
        parts = parts + [first[index]] + [flip(part, bit) for part in parts[1:]]
    return parts


def half_rest(low, sent):
    for bit in range(1, axis_bits("tensor")):
        low = add_rows(low, sent)
        sent = flip(low, bit)
    return low, sent


def gather_half(half):
    return [half, flip(half, 0)]


def to_second(value):
    return lax.ppermute(value, "section", [(0, 1)])


def to_first(value):
    return lax.ppermute(value, "section", [(1, 0)])


def sum_over(value, axis):
    for bit in range(axis_bits(axis)):
        value = value + flip(value, bit, axis)
    return value


def table_rows_of(value, table, tables, half):
    return jnp.concatenate([value[(core * tables + table) * half : (core * tables + table + 1) * half] for core in range(2)], axis=0)


def in_frame(values, half):
    return jnp.concatenate([value[core * half : (core + 1) * half] for core in range(2) for value in values], axis=0)


def decoder_attend(q, keys, values, masks, w_out, outs):
    heads_out, wide_out, log_out, low, high = outs
    tables = len(keys)
    half = q.shape[0] // (2 * tables)
    wides = []
    for table in range(tables):
        wide, logs = attention_rows(table_rows_of(q, table, tables, half), keys[table], values[table], masks[table])
        wides.append(wide)
        log_out[table * 8 : table * 8 + 8] = logs[:8]
    wide = in_frame(wides, half)
    heads = wide.astype(bf16)
    wide_out[...] = wide
    heads_out[...] = heads
    partial = mm_t(heads, w_out).astype(bf16)
    low[...] = partial[: tables * half]
    high[...] = partial[tables * half :]


def attend_shapes(rows, columns, width, tables):
    shapes = [(rows, columns, bf16), (rows, columns, f32), (8 * tables, rows // tables, f32), (rows // 2, width, bf16), (rows // 2, width, bf16)]
    return [full(shape[:2]) for shape in shapes], [shaped(*shape) for shape in shapes]


def decoder_self(parts, w_q, w_k, w_v, bias, masks, w_out):
    tables = masks.shape[0]
    rows, width = 2 * parts[0].shape[0], parts[0].shape[1]
    half = rows // (2 * tables)
    columns = w_q.shape[1]

    def kernel(own, other, w_q, w_k, w_v, bias, masks, w_out, x_out, q_out, k_out, v_out, *outs):
        x = jnp.concatenate([own[...], other[...]], axis=0)
        x_out[...] = x
        q = (mm(x, w_q[...]) + bias[0:1]).astype(bf16)
        k = mm(x, w_k[...]).astype(bf16)
        v = (mm(x, w_v[...]) + bias[1:2]).astype(bf16)
        q_out[...], k_out[...], v_out[...] = q, k, v
        keys, values = ([table_rows_of(value, table, tables, half) for table in range(tables)] for value in (k, v))
        decoder_attend(q, keys, values, [masks[table] for table in range(tables)], w_out[...], outs)

    specs, shapes = attend_shapes(rows, columns, width, tables)
    return call(
        kernel, (1,),
        [full(value.shape) for value in (*parts, w_q, w_k, w_v, bias, masks, w_out)],
        [full((rows, width))] + [full((rows, columns))] * 3 + specs,
        [shaped(rows, width)] + [shaped(rows, columns)] * 3 + shapes, [],
        cost(8 * rows * width * columns, 8 * width * columns),
        *parts, w_q, w_k, w_v, bias, masks, w_out,
    )


def decoder_cross(parts, w_q, bias, keys, values, masks, w_out):
    tables = len(keys)
    rows, width = 2 * parts[0].shape[0], parts[0].shape[1]
    columns = w_q.shape[1]

    def kernel(own, other, w_q, bias, masks, w_out, *refs):
        keys, values, (x_out, q_out), outs = refs[:tables], refs[tables : 2 * tables], refs[2 * tables : 2 * tables + 2], refs[2 * tables + 2 :]
        x = jnp.concatenate([own[...], other[...]], axis=0)
        x_out[...] = x
        q = (mm(x, w_q[...]) + bias[...]).astype(bf16)
        q_out[...] = q
        decoder_attend(q, keys, values, [masks[table : table + 1] for table in range(tables)], w_out[...], outs)

    specs, shapes = attend_shapes(rows, columns, width, tables)
    return call(
        kernel, (1,),
        [full(value.shape) for value in (*parts, w_q, bias, masks, w_out, *keys, *values)],
        [full((rows, width)), full((rows, columns))] + specs,
        [shaped(rows, width), shaped(rows, columns)] + shapes, [],
        cost(4 * rows * width * columns + 4 * rows * keys[0].shape[0] * columns, 8 * width * columns),
        *parts, w_q, bias, masks, w_out, *keys, *values,
    )


def decoder_attend_back(grads, wide, logs, q, keys, values, masks):
    tables = len(keys)
    half = q.shape[0] // (2 * tables)
    dqs, dks, dvs = [], [], []
    for table in range(tables):
        dk_parts, dv_parts = [], []

        def add(at, dk, dv):
            dk_parts.append(dk.astype(bf16))
            dv_parts.append(dv.astype(bf16))

        g, w, q_rows = (table_rows_of(value, table, tables, half) for value in (grads, wide, q))
        dqs.append(attention_back_rows(g, w, logs[table * 8 : table * 8 + 8], q_rows, keys[table], values[table], masks[table], add))
        dks.append(jnp.concatenate(dk_parts, axis=1))
        dvs.append(jnp.concatenate(dv_parts, axis=1))
    return in_frame(dqs, half), dks, dvs


def rows_sum(value):
    return jnp.sum(value.astype(f32), axis=0, keepdims=True)


def decoder_cross_back(parts, w_out, wide, logs, q, keys, values, masks, w_q):
    tables = len(keys)
    rows, width = 2 * parts[0].shape[0], parts[0].shape[1]
    columns = w_q.shape[1]
    slots = keys[0].shape[0]

    def kernel(own, other, w_out, wide, logs, q, masks, w_q, *refs):
        keys, values, outs = refs[:tables], refs[tables : 2 * tables], refs[2 * tables :]
        x = jnp.concatenate([own[...], other[...]], axis=0)
        outs[0][...] = x
        grads = mm(x, w_out[...]).astype(bf16)
        columns_of = [masks[:, table : table + 1] for table in range(tables)]
        dq, dks, dvs = decoder_attend_back(grads, wide[...], logs[...], q[...], keys, values, columns_of)
        outs[1][...] = dq
        outs[2][...] = rows_sum(dq)
        partial = mm_t(dq, w_q[...]).astype(bf16)
        outs[3][...] = partial[: rows // 2]
        outs[4][...] = partial[rows // 2 :]
        total = 0.0
        for table in range(tables):
            outs[6 + table][...] = dks[table]
            outs[6 + tables + table][...] = dvs[table]
            total = total + rows_sum(dvs[table])
        outs[5][...] = total

    shapes = [(rows, width, bf16), (rows, columns, bf16), (1, columns, f32), (rows // 2, width, bf16), (rows // 2, width, bf16), (1, columns, f32)]
    shapes += [(slots, columns, bf16)] * (2 * tables)
    return call(
        kernel, (1,),
        [full(value.shape) for value in (*parts, w_out, wide, logs, q, masks, w_q, *keys, *values)],
        [full(shape[:2]) for shape in shapes], [shaped(*shape) for shape in shapes], [],
        cost(4 * rows * width * columns + 10 * rows * slots * columns, 8 * width * columns),
        *parts, w_out, wide, logs, q, masks, w_q, *keys, *values,
    )


def decoder_self_back(parts, w_out, wide, logs, q, k, v, masks, w_q, w_k, w_v):
    tables = masks.shape[0]
    rows, width = 2 * parts[0].shape[0], parts[0].shape[1]
    half = rows // (2 * tables)
    columns = w_q.shape[1]

    def kernel(own, other, w_out, wide, logs, q, k, v, masks, w_q, w_k, w_v, x_out, q_out, k_out, v_out, q_sum, v_sum, low, high):
        x = jnp.concatenate([own[...], other[...]], axis=0)
        x_out[...] = x
        grads = mm(x, w_out[...]).astype(bf16)
        keys, values = ([table_rows_of(value[...], table, tables, half) for table in range(tables)] for value in (k, v))
        dq, dks, dvs = decoder_attend_back(grads, wide[...], logs[...], q[...], keys, values, [masks[table] for table in range(tables)])
        dk, dv = in_frame(dks, half), in_frame(dvs, half)
        q_out[...], k_out[...], v_out[...] = dq, dk, dv
        q_sum[...], v_sum[...] = rows_sum(dq), rows_sum(dv)
        partial = (mm_t(dq, w_q[...]) + mm_t(dk, w_k[...]) + mm_t(dv, w_v[...])).astype(bf16)
        low[...] = partial[: rows // 2]
        high[...] = partial[rows // 2 :]

    shapes = [(rows, width, bf16)] + [(rows, columns, bf16)] * 3 + [(1, columns, f32)] * 2 + [(rows // 2, width, bf16)] * 2
    return call(
        kernel, (1,),
        [full(value.shape) for value in (*parts, w_out, wide, logs, q, k, v, masks, w_q, w_k, w_v)],
        [full(shape[:2]) for shape in shapes], [shaped(*shape) for shape in shapes], [],
        cost(12 * rows * width * columns, 8 * width * columns),
        *parts, w_out, wide, logs, q, k, v, masks, w_q, w_k, w_v,
    )


def per_device(
    table_input,
    target_input,
    cotangent,
    table_lengths,
    target_lengths,
    query_key,
    value_out,
    hidden_in,
    hidden_out,
    hidden_bias,
    vectors,
    cross_bias,
):
    sections = lax.axis_size("section")
    count = lax.axis_size("tensor")
    bits = axis_bits("tensor")
    rank = lax.axis_index("tensor")
    section = lax.axis_index("section")
    is_first = section == 0
    section_ref = section.reshape(1).astype(jnp.int32)
    in_line = lax.axis_size("dp") == CHUNKS
    place = lax.axis_index("dp")
    beyond = jnp.logical_and(in_line, place >= CHUNKS // 2).astype(jnp.int32)
    inner = jnp.where(in_line, ((place == 1) | (place == 2)).astype(jnp.int32), 1)
    line_ref = jnp.stack([beyond, inner])
    order_ref = (jnp.arange(CHUNKS, dtype=jnp.int32) + beyond * (CHUNKS // 2)) % CHUNKS
    place_ref = jnp.where(in_line, lax.axis_index("dp"), 0).reshape(1).astype(jnp.int32)
    tables, slots, width = table_input.shape
    targets = target_input.shape[1]
    columns = query_key.shape[3]
    rows = vectors[0]
    row = [rows[index : index + 1] for index in range(rows.shape[0])]
    head_rows = lax.dynamic_slice_in_dim(rows[0:3], rank * columns, columns, 1)
    no_bias = jnp.zeros((1, columns), f32)
    w_query, w_key, w_third_q = query_key[0, 0], query_key[0, 1], query_key[0, 2]
    w_value, w_out, w_third_v = value_out[0, 0], value_out[0, 1], value_out[0, 2]
    w_in, w_hidden_out = hidden_in[0], hidden_out[0]

    masks = [int(format(p, f"0{bits}b")[::-1], 2) for p in range(count)]
    owners = rank.astype(jnp.int32) ^ jnp.array(masks, jnp.int32)
    short = slots // (sections * count)
    row_index = (
        jnp.arange(sections)[None, :, None] * (count * short)
        + owners[:, None, None] * short
        + jnp.arange(short)[None, None, :]
    ).reshape(-1)
    table_valid = row_index[None, :] < table_lengths[:, None]
    table_mask = jnp.where(table_valid, 0.0, -1e30).astype(f32)

    cores = 2
    small = targets // (sections * count)
    core_order = (rank % cores) ^ jnp.arange(cores)
    half = targets // cores

    def target_frame(value):
        split = value.reshape(tables, sections, count // cores, cores, small, width)
        split = jnp.take(split, core_order, axis=3)
        return jnp.transpose(split, (3, 0, 2, 1, 4, 5)).reshape(cores, tables * half, width)

    target_index = (
        jnp.arange(sections)[None, None, :, None] * (count * small)
        + jnp.arange(count // cores)[None, :, None, None] * (cores * small)
        + core_order[:, None, None, None] * small
        + jnp.arange(small)[None, None, None, :]
    ).reshape(-1)
    target_rows = target_frame(target_input)
    grad_rows_half = target_frame(cotangent)[0]
    target_valid = target_index[None, :] < target_lengths[:, None]
    causal = (target_index[None, :] <= target_index[:, None])[None] & target_valid[:, None, :]

    causal_mask = jnp.where(causal, 0.0, -1e30).astype(f32)
    causal_back = jnp.swapaxes(causal_mask, 1, 2)

    encoder_kept, encoder_out = {}, {}
    cross, dec, grad_memory = {}, {}, {}
    w_cross_key = w_cross_value = b_cross_value = None
    order.last = None

    def encode(table):
        first_in, queries, keys, values, normed, raw = encoder_qkv(
            table_input, table, owners, row[9], row[10], w_query, w_key, w_value, head_rows[0:2], sections
        )
        yield "qkv"
        heads, wide, logs, low, high = encoder_attention(queries, keys, values, table_mask[table][None], w_out, count)
        sent = flip(high, 0)
        yield "attention"
        parts = reduce_rest(low, sent)
        yield "reduce"
        summed_one, middle, sent = norm_forward(normed, parts, row[3], row[5], row[6])
        started = gather_start(sent)
        yield "norm"
        parts = gather_rest(started)
        yield "gather"
        second_in, hidden, slope, low, high = ffn_forward(parts, w_in, hidden_bias, w_hidden_out)
        sent = flip(high, 0)
        yield "ffn"
        parts = reduce_rest(low, sent)
        yield "reduce two"
        summed_two, _, memory = norm_forward(middle, parts, row[4], row[7], row[8])
        encoder_kept[table] = (raw, first_in, queries, keys, values, heads, wide, logs, summed_one, second_in, hidden, slope, summed_two)
        memory = to_second(memory)
        yield "memory"
        started = gather_start(memory)
        yield "moved"
        yield "gather two"
        cross[table] = project_parts(gather_rest(started), [w_cross_key, w_cross_value], [no_bias, b_cross_value])
        yield "cross"

    def decode():
        dec["first"], q, k, v, heads, wide, logs, low, high = decoder_self(
            [target_rows[0], target_rows[1]], w_query, w_key, w_value, head_rows[0:2], causal_mask, w_out
        )
        dec["self"] = (q, k, v, heads, wide, logs)
        sent = flip(high, 0)
        yield "self"
        parts = half_rest(low, sent)
        yield "reduce"
        dec["one"], middle, sent = norm_forward(target_rows[0].astype(f32), parts, row[3], row[5], row[6])
        sent = gather_half(sent)
        yield "norm"
        keys, values = [cross[table][1] for table in range(tables)], [cross[table][2] for table in range(tables)]
        cross_in, q, heads, wide, logs, low, high = decoder_cross(
            sent, w_third_q, head_rows[2:3], keys, values, table_mask, w_third_v
        )
        parts = half_rest(low, flip(high, 0))
        three, later, sent = norm_forward(middle, parts, cross_bias[None], row[9], row[10])
        third_in, hidden, slope, low, high = ffn_forward(gather_half(sent), w_in, hidden_bias, w_hidden_out)
        parts = half_rest(low, flip(high, 0))
        two, _, dec["out"] = norm_forward(later, parts, row[4], row[7], row[8])
        grad_two, sent, dec["sums_two"] = norm_backward(two, row[7], [grad_rows_half])
        grad_two_rows, before_grad, low, high, dec["bias"] = ffn_backward(gather_half(sent), slope, w_in, w_hidden_out)
        parts = half_rest(low, flip(high, 0))
        grad_three, sent, dec["sums_three"] = norm_backward(three, row[9], [grad_two, *parts])
        grad_three_rows, dq, dec["third_sum"], low, high, third_bias, *rest = decoder_cross_back(
            gather_half(sent), w_third_v, wide, logs, q, keys, values, jnp.swapaxes(table_mask, 0, 1), w_third_q
        )
        dec["cross_rows"] = low, high
        dks, dvs = rest[:tables], rest[tables:]
        for table in range(tables):
            low, high = back_sum([dks[table], dvs[table]], [w_cross_key, w_cross_value], count)
            dec["memory", table] = low, flip(high, 0)
        dec["grad_three"] = grad_three
        dec["pairs"] = {"in": [(third_in, before_grad)], "out": [(grad_two_rows, hidden)]}
        yield "back"
        memory_rows = [cross[table][0] for table in range(tables)]
        arrived = weight_sum(memory_rows, dks), weight_sum(memory_rows, dvs)
        own = weight_sum([cross_in], [dq]), weight_sum([grad_three_rows], [heads])
        yield "thirds"
        arrived = [to_first(value) for value in gate(*arrived)]
        dec["third_bias"] = to_first(third_bias)
        yield "third send"
        first, *rest = pick_third(section_ref, place_ref, arrived, own)
        if in_line:
            sent = send_chunks(rest)
        yield "third pick"
        if in_line:
            total = sum_chunks(first, sent)
            sent = send_chunks([total] * (CHUNKS - 1))
            dec["thirds"] = [total, *sent]
        else:
            totals = lax.psum([first, *rest], "dp")
            dec["thirds"] = totals[:1] + totals[:0:-1]
        yield "third sum"
        dec["thirds"] = gate(*dec["thirds"])
        yield "third end"

    def memory_back(table):
        keep, sent = reduce_rest(*dec["memory", table])
        yield "reduce"
        grad_memory[table] = to_first(add_rows(keep, sent))
        yield "moved"

    def decode_rest():
        low, high = gate(*dec["cross_rows"])
        sent = flip(high, 0)
        yield "start"
        parts = half_rest(low, sent)
        yield "reduce"
        grad_one, sent, dec["sums_one"] = norm_backward(dec["one"], row[5], [dec["grad_three"], *parts])
        sent = gather_half(sent)
        yield "norm"
        q, k, v, heads, wide, logs = dec["self"]
        grad_one_rows, grad_q, grad_k, grad_v, dec["sum_q"], dec["sum_v"], low, high = decoder_self_back(
            sent, w_out, wide, logs, q, k, v, causal_back, w_query, w_key, w_value
        )
        first = dec["first"]
        dec["pairs"].update({"qk": [(first, grad_q), (first, grad_k)], "vo": [(first, grad_v), (grad_one_rows, heads)]})
        sent = flip(high, 0)
        yield "self"
        keep, sent = half_rest(low, sent)
        yield "reduce two"
        dec["target_grad"] = (grad_one + keep.astype(f32) + sent.astype(f32)).astype(bf16)

    def encode_back(table):
        (raw, first_in, queries, keys, values, heads, wide, logs, summed_one, second_in, hidden, slope, summed_two) = encoder_kept[table]
        grad_two, sent, sums_two = norm_backward(summed_two, row[7], [grad_memory[table]])
        started = gather_start(sent)
        yield "norm two"
        parts = gather_rest(started)
        pairs = encoder_out[table] = {"out": [(tuple(parts), hidden)]}
        yield "gather two"
        _, grad_before, low, high, bias = ffn_backward(parts, slope, w_in, w_hidden_out)
        pairs["in"] = [(second_in, grad_before)]
        sent = flip(high, 0)
        yield "ffn"
        parts = reduce_rest(low, sent)
        yield "reduce two"
        grad_one, sent, sums_one = norm_backward(summed_one, row[5], [grad_two, *parts])
        started = gather_start(sent)
        yield "norm one"
        yield "gather one"
        grad_one_rows, grad_q, grad_k, grad_v, sum_q, sum_v = encoder_attention_back(
            gather_rest(started), wide, logs, queries, keys, values, table_mask[table][:, None], w_out
        )
        pairs.update({"qk": [(first_in, grad_q), (first_in, grad_k)], "vo": [(first_in, grad_v), (grad_one_rows, heads)]})
        yield "attention"
        low, high = back_sum([grad_q, grad_k, grad_v], [w_query, w_key, w_value], count)
        sent = flip(high, 0)
        yield "back"
        parts = reduce_rest(low, sent)
        yield "reduce one"
        _, pairs["table_grad"], sums_zero = norm_backward(raw, row[9], [grad_one, *parts])
        pairs["sums"] = (sums_one, sums_two, sums_zero, sum_q, sum_v, bias)
        yield "norm zero"

    totals = {}

    def weights(name):
        totals[name] = []
        rows = weight_grad(section_ref, order_ref, [encoder_out[table][name] for table in range(tables)], dec["pairs"][name])
        yield from sum_line(rows, totals[name])
        if name in ("out", "in"):
            totals[name] = unite_one(line_ref, totals[name])
            yield "four"

    def cross_weights():
        nonlocal w_cross_key, w_cross_value, b_cross_value
        sent = gate(w_third_q, w_third_v, head_rows[2:3])
        w_cross_key, w_cross_value, b_cross_value = (to_second(value) for value in sent)
        yield "send"
        w_cross_key, w_cross_value, b_cross_value = gate(w_cross_key, w_cross_value, b_cross_value)
        yield "gate"

    parts = {"d": decode(), "g": cross_weights(), "r": decode_rest()}
    for table in range(tables):
        parts[f"e{table}"] = encode(table)
        parts[f"m{table}"] = memory_back(table)
        parts[f"b{table}"] = encode_back(table)
    for name in ("out", "in", "qk", "vo"):
        parts[name] = weights(name)
    for name, label in ORDER:
        for said in parts[name]:
            if said == label:
                break
    for part in parts.values():
        for _ in part:
            pass

    table_grads = [encoder_out[table]["table_grad"] for table in range(tables)]
    decoded, target_grad = dec["out"], dec["target_grad"]
    total_out, total_in = totals["out"], totals["in"]

    bundle = vector_rows(
        section_ref,
        rank.reshape(1).astype(jnp.int32),
        [encoder_out[table]["sums"] for table in range(tables)],
        dec["third_bias"],
        [dec[name] for name in ("sums_one", "sums_two", "sums_three", "sum_q", "sum_v", "third_sum", "bias")],
        cores / count,
    )
    bundle = sum_over(bundle, "dp")
    query_key_grad, value_out_grad = unite(place_ref, line_ref, totals["qk"], totals["vo"], dec["thirds"])
    bias_sum = bundle[12:13, : w_in.shape[1]]
    bundle = sum_over(bundle, "tensor")
    vector_total = bundle[:11]
    cross_total = bundle[11] + lax.ppermute(bundle[11], "section", [(0, 1), (1, 0)])

    table_grads = jnp.stack(table_grads).reshape(tables, sections, short, width)
    moved_up = lax.ppermute(table_grads[:, 1], "section", [(0, 1)])
    table_out = jnp.where(is_first, table_grads[:, 0], moved_up)
    own = lax.dynamic_slice_in_dim(
        jnp.stack([decoded, target_grad]).reshape(2, tables, count // cores, sections, small, width),
        rank // cores,
        1,
        2,
    )[:, :, 0]
    moved_down = lax.ppermute(own[:, :, 0], "section", [(1, 0)])
    small_out = jnp.where(is_first, moved_down, own[:, :, 1])
    return (
        small_out[0],
        table_out,
        small_out[1],
        query_key_grad[None],
        value_out_grad[None],
        total_in[None],
        total_out[None],
        bias_sum,
        vector_total[None],
        cross_total,
    )


def solution(mesh):
    in_specs = (
        P("dp", None, None),
        P("dp", None, None),
        P("dp", None, None),
        P("dp"),
        P("dp"),
        P("section", None, None, "tensor"),
        P("section", None, None, "tensor"),
        P("section", None, "tensor"),
        P("section", None, "tensor"),
        P("section", "tensor"),
        P("section", None, None),
        P(),
    )
    out_specs = (
        P("dp", ("section", "tensor"), None),
        P("dp", ("section", "tensor"), None),
        P("dp", ("section", "tensor"), None),
        P("section", None, None, "tensor"),
        P("section", None, None, "tensor"),
        P("section", None, "tensor"),
        P("section", None, "tensor"),
        P("section", "tensor"),
        P("section", None, None),
        P(),
    )
    return jax.shard_map(
        per_device, mesh=mesh, in_specs=in_specs, out_specs=out_specs, check_vma=False
    )
```
